512 devices in a mesh: depth: 16 (over z, core), tile: 32 (over x, y).
Axes of the slice: x: 4, y: 8, z: 8, core: 2. Of those that a mesh axis runs over, the one named last changes fastest.
Arguments:
- bricks: bfloat16 [16, 512, 32, 1024], P('depth', 'tile'), may hold values from -8 to 8
- levels: int32 [16, 512], P('depth', 'tile'), may hold values from 0 to 2
- counts: int32 [16, 512, 1024], P('depth', 'tile'), may hold values from 1 to 32
- gains: float32 [16, 512], P('depth', 'tile'), may hold values from 0.002 to 0.03
- ownership: int32 [16, 32, 16], P('depth'), may hold values from 0 to 31, as said below
- tf_slope: float32 [3], replicated, may hold values from 0.5 to 3
Outputs:
- rgba: float32 [4, 16, 32768], P(None, 'depth', 'tile')
- work_share: float32 [16, 32], P('depth', 'tile')
The draws below stay inside these ranges and needn't reach their ends.
Inputs may be any that keep to these rules, and one draw needn't show every extreme that they name: `ownership`: slot j of tile t in depth slab d belongs to tile (t + s) mod 32, where the shift s depends on d and j only; two slots share a shift only when j - j' is a multiple of 32. So every device renders exactly 16 bricks and takes exactly 1 bricks from each device that sends it any.
All inputs are finite; a program needn't handle non-finite values.
Results may differ from the reference program's by a relative error of at most 0.0034.
Values may be sent and summed in bfloat16 or wider, within the bound.
A program may use at most 64 MiB of HBM per device.

```python
import math
import jax
import jax.numpy as jnp
from jax import lax

BS = 32
BRICK_DEV = 16
BRICKS = 512
PIXELS = 524288
N_DEPTH = 16
N_TILE = 32


def draw_levels(key, part):
    first_key, second_key = jax.random.split(jax.random.fold_in(key, 11))
    hot_tile = jax.random.randint(first_key, (N_DEPTH, N_TILE, 1), 0, 4) == 0
    base_draw = jax.random.randint(second_key, (N_DEPTH, N_TILE, BRICK_DEV), 0, 4)
    coarse_level = jnp.where(base_draw < 2, 0, base_draw - 1)
    chosen = jnp.where(hot_tile, 2, coarse_level)
    return chosen.reshape(N_DEPTH, N_TILE * BRICK_DEV).astype(jnp.int32)


def draw_ownership(key, part):
    row_keys = jax.random.split(jax.random.fold_in(key, 23), N_DEPTH)
    shuffles = jax.vmap(lambda row_key: jax.random.permutation(row_key, N_TILE))(row_keys)
    slot_ids = jnp.arange(BRICK_DEV, dtype=jnp.int32) % N_TILE
    shifts = shuffles[:, slot_ids]
    tile_ids = jnp.arange(N_TILE, dtype=jnp.int32)
    owners = (tile_ids[None, :, None] + shifts[:, None, :]) % N_TILE
    return owners.astype(jnp.int32)


def with_ends(array, rng, least, top_value):
    dims = array.shape
    spot = [jax.random.randint(jax.random.fold_in(rng, axis), (), 0, dims[axis]) for axis in range(len(dims))]
    array = array.at[tuple(spot)].set(least)
    longest = dims.index(max(dims))
    spot[longest] = (spot[longest] + 1) % dims[longest]
    return array.at[tuple(spot)].set(top_value)


def level_of(rng, dims, shards, least, high):
    gain = 1.0
    for axis_at, parts in shards:
        steps = jax.random.uniform(jax.random.fold_in(jax.random.fold_in(rng, 6), axis_at), (parts,), jnp.float32, least / len(shards), high / len(shards))
        gain = gain * jnp.repeat(jnp.exp(steps), dims[axis_at] // parts).reshape((-1,) + (1,) * (len(dims) - 1 - axis_at))
    return gain


def scatter_about(own_key, extent, spread, bound, pieces=(), held_as=jnp.bfloat16):
    values = jax.random.normal(own_key, extent, jnp.float32) * spread
    if len(pieces) > 0:
        values = level_of(own_key, extent, pieces, -0.22, 0.18) * values
    return jnp.clip(values, min=-bound, max=bound).astype(held_as)


def setup_inputs(seed: int = 0) -> dict:
    key_list = jax.random.split(jax.random.key(seed), 7)
    bricks = scatter_about(key_list[0], (N_DEPTH, BRICKS, BS, BS * BS), 1.5, 8.0, ((0, 16), (1, 32)))
    levels = draw_levels(jax.random.fold_in(key_list[6], 71), 0)
    counts = with_ends(jax.random.randint(key_list[2], (N_DEPTH, BRICKS, BS * BS), 1, BS + 1), jax.random.fold_in(key_list[2], 1), 1, BS).astype(jnp.int32)
    gains = jnp.clip(jnp.exp(math.log(0.03) - 2.70805 * jax.random.uniform(key_list[3], (N_DEPTH, BRICKS), jnp.float32) ** level_of(key_list[3], (N_DEPTH, BRICKS), ((0, 16), (1, 32)), -0.2, 0.2)), 0.002, 0.03)
    ownership = draw_ownership(jax.random.fold_in(key_list[6], 71), 0)
    tf_slope = jnp.clip(jax.random.uniform(key_list[5], (3,), jnp.float32, 0.5, 3.0), 0.5, 3.0)
    return dict(bricks=bricks, levels=levels, counts=counts, gains=gains, ownership=ownership, tf_slope=tf_slope)


def tent_tables(brick_side):
    cell_index = jnp.arange(brick_side, dtype=jnp.float32)
    tables = []
    for level_index in range(3):
        coarse_cells = brick_side * (2 ** level_index) // 4
        coarse_at = jnp.clip((cell_index + 0.5) * (coarse_cells / brick_side) - 0.5, 0.0, coarse_cells - 1.0)
        tables.append(jnp.maximum(0.0, 1.0 - jnp.abs(coarse_at[:, None] - cell_index[None, :])))
    return jnp.stack(tables)


def level_worth(level_grid):
    return jnp.where(level_grid == 2, 1.0, jnp.where(level_grid == 1, 0.25, 0.0625)).astype(jnp.float32)


def reference(bricks, levels, counts, gains, ownership, tf_slope):
    tent_rows = tent_tables(BS)
    highest = lax.Precision.HIGHEST

    def one_row(packed):
        row_bricks, row_levels, row_counts, row_gains = packed
        tent_each = tent_rows[row_levels]
        cube = row_bricks.astype(jnp.float32).reshape(-1, BS, BS, BS)
        along_x = jnp.einsum('bxe,bzye->bzyx', tent_each, cube, precision=highest)
        along_y = jnp.einsum('byc,bzcx->bzyx', tent_each, along_x, precision=highest)
        density = jnp.einsum('bza,bayx->bzyx', tent_each, along_y, precision=highest).reshape(-1, BS, BS * BS)
        softened = jax.nn.softplus(density)
        depth_index = jnp.arange(BS, dtype=jnp.int32)
        live_mask = depth_index[None, :, None] < row_counts[:, None, :]
        optical = row_gains[:, None, None] * jnp.where(live_mask, softened, 0.0)
        optical_before = jnp.cumsum(optical, axis=1) - optical
        emission = jnp.exp(-optical_before) * (1.0 - jnp.exp(-optical))
        channels = jnp.stack([jnp.sum(emission * jax.nn.sigmoid(tf_slope[k] * density), axis=1) for k in range(3)], axis=1)
        slab_pass = jnp.exp(-(optical_before[:, -1] + optical[:, -1]))
        return channels, slab_pass

    colors, passes = lax.map(one_row, (bricks, levels, counts, gains))
    colors = jnp.transpose(colors, (0, 2, 1, 3)).reshape(N_DEPTH, 3, PIXELS)
    passes = passes.reshape(N_DEPTH, PIXELS)
    in_front = jnp.concatenate([jnp.ones((1, PIXELS), jnp.float32), jnp.cumprod(passes, axis=0)[:-1]], axis=0)
    color_sum = jnp.sum(in_front[:, None, :] * colors, axis=0)
    opacity = 1.0 - jnp.prod(passes, axis=0)
    stacked = jnp.concatenate([color_sum, opacity[None, :]], axis=0)
    rgba = jnp.transpose(stacked.reshape(4, PIXELS // N_DEPTH, N_DEPTH), (0, 2, 1))
    owner_flat = ownership.reshape(N_DEPTH, BRICKS)
    tile_ids = jnp.arange(N_TILE, dtype=jnp.int32)
    chosen = (owner_flat[:, :, None] == tile_ids[None, None, :]).astype(jnp.float32)
    work_share = jnp.sum(level_worth(levels)[:, :, None] * chosen, axis=1) / BRICK_DEV
    return rgba, work_share
```

```python
import functools

import jax
import jax.numpy as jnp
from jax import lax
from jax.experimental import pallas as pl
from jax.experimental.pallas import tpu as pltpu
from jax.sharding import PartitionSpec as P

F32 = jnp.float32
BF16 = jnp.bfloat16
I32 = jnp.int32
MESH = pl.DeviceIdType.MESH


def tent(at, cell):
    return jnp.maximum(0.0, 1.0 - jnp.abs(at - cell))


def coarse_at(fine, side):
    return jnp.clip((fine + 0.5) * (side / 32.0) - 0.5, 0.0, side - 1.0)


def fill_plane_maps(maps):
    lane = lax.broadcasted_iota(I32, (8, 1024), 1)
    y_of = (lane // 32).astype(F32)
    x_of = lax.broadcasted_iota(I32, (32, 128), 1) % 32
    e_of = lax.broadcasted_iota(I32, (32, 128), 0).astype(F32)
    for first, side in ((0, 8), (256, 16)):
        along_x = tent(coarse_at(x_of.astype(F32), side), e_of)
        along_x = jnp.concatenate([along_x] * 8, axis=1)
        y_at = coarse_at(y_of, side)

        def one(c, carry, first=first, along_x=along_x, y_at=y_at):
            along_y = tent(y_at, c.astype(F32))
            both = along_x * jnp.concatenate([along_y] * 4, axis=0)
            maps[pl.ds(pl.multiple_of(first + c * 32, 32), 32), :] = both.astype(BF16)
            return carry

        lax.fori_loop(0, side, one, 0)


def depth_map(levels, half):
    lane = lax.broadcasted_iota(I32, (1, 256), 1)
    slot = lane // 32
    grade = jnp.zeros((1, 256), I32)
    for s in range(8):
        grade = jnp.where(slot == s, levels[0, 2 * s + half], grade)
    side = jnp.where(grade == 2, 32.0, jnp.where(grade == 1, 16.0, 8.0))
    cell = lane % 32
    cell = jnp.where(grade == 2, cell, cell % 16).astype(F32)
    row = lax.broadcasted_iota(I32, (256, 256), 0)
    z_of = (row // 8).astype(F32)
    at = jnp.minimum(jnp.maximum((z_of + 0.5) * (side / 32.0) - 0.5, 0.0), side - 1.0)
    same = (row % 8) == (lax.broadcasted_iota(I32, (256, 256), 1) // 32)
    return jnp.where(same, tent(at, cell), 0.0).astype(BF16)


def kernel(
    depth_count, x_count, y_count,
    bricks, levels, counts, gains, owners, slope,
    out, share,
    raw, lives, masked, maps, cells, zmaps, dens, shaded, sends, boxes, mine, other,
    row_send, row_got, block_send, block_got,
    brick_sem, live_sem, send_sem, box_sem, pair_sem, row_sems, row_box, block_sems, block_box,
):
    me = lax.axis_index("depth")
    tile = lax.axis_index("tile")
    chip, core = me // 2, me % 2
    chips = depth_count // 2
    my_x, my_y = tile // y_count, tile % y_count

    fetch_bricks = [
        pltpu.make_async_copy(bricks.at[0, pl.ds(i * 8, 8)], raw.at[pl.ds(i * 8, 8)], brick_sem.at[i])
        for i in range(2)
    ]
    fetch_lives = [
        pltpu.make_async_copy(counts.at[0, :, pl.ds(j * 128, 128)], lives.at[j], live_sem.at[j])
        for j in range(8)
    ]
    for copy in fetch_bricks + fetch_lives:
        copy.start()

    barrier = pltpu.get_barrier_semaphore()

    def greet_depth(hop, carry):
        pl.semaphore_signal(barrier, inc=1, device_id={"depth": lax.rem(me + hop, depth_count)}, device_id_type=MESH)
        return carry

    lax.fori_loop(1, depth_count, greet_depth, 0)
    for hop in range(1, y_count):
        there = my_x * y_count + lax.rem(my_y + hop, y_count)
        pl.semaphore_signal(barrier, inc=1, device_id={"tile": there}, device_id_type=MESH)
    for hop in range(1, x_count):
        there = lax.rem(my_x + hop, x_count) * y_count + my_y
        pl.semaphore_signal(barrier, inc=1, device_id={"tile": there}, device_id_type=MESH)

    fill_plane_maps(maps)
    for half in range(2):
        zmaps[half] = depth_map(levels, half)

    for copy in fetch_bricks:
        copy.wait()
    for slot in range(16):
        b = 2 * (slot % 8) + slot // 8
        grade = levels[0, b]
        rows = pl.ds(slot * 16, 16)
        for first, width, wanted in ((0, 256, 0), (256, 512, 1)):
            keep = jnp.full((16, width), jnp.where(grade == wanted, 1.0, 0.0), F32).astype(BF16)
            masked[rows, first : first + width] = raw[b, 0:16, 0:width] * keep

    for n in range(4):
        lanes = pl.ds(n * 256, 256)
        plane = jnp.dot(masked[...], maps[:, lanes], preferred_element_type=F32)
        high = plane.astype(BF16)
        low = (plane - high.astype(F32)).astype(BF16)
        for slot in range(16):
            b = 2 * (slot % 8) + slot // 8
            keep = jnp.full((16, 256), jnp.where(levels[0, b] == 2, 1.0, 0.0), F32).astype(BF16)
            here = slice(slot * 16, slot * 16 + 16)
            cells[pl.ds(slot * 32, 16), lanes] = raw[b, 0:16, lanes] * keep + high[here]
            cells[pl.ds(slot * 32 + 16, 16), lanes] = raw[b, 16:32, lanes] * keep + low[here]

    for half in range(2):
        for n in range(4):
            lanes = pl.ds(n * 256, 256)
            dens[half, :, lanes] = jnp.dot(
                zmaps[half], cells[pl.ds(half * 256, 256), lanes], preferred_element_type=F32
            )

    pl.semaphore_wait(barrier, depth_count - 1 + y_count - 1 + x_count - 1)

    sub = lax.broadcasted_iota(I32, (8, 128), 0)
    lane = lax.broadcasted_iota(I32, (8, 128), 1)
    level_row = jnp.zeros((8, 128), I32)
    for b in range(16):
        level_row = jnp.where(lane == b, levels[0, b], level_row)
    row_send[...] = level_row
    row_got[my_y] = level_row
    row_copies = []
    for hop in range(1, y_count):
        there = my_x * y_count + lax.rem(my_y + hop, y_count)
        copy = pltpu.make_async_remote_copy(
            src_ref=row_send, dst_ref=row_got.at[my_y],
            send_sem=row_sems.at[hop], recv_sem=row_box.at[my_y],
            device_id={"tile": there}, device_id_type=MESH,
        )
        copy.start()
        row_copies.append(copy)

    for copy in fetch_lives:
        copy.wait()
    slopes = [slope[k] * 0.5 for k in range(3)]
    sends_started = []
    block_copies = []
    for half in range(2):
        gain = jnp.zeros((8, 128), F32)
        for s in range(8):
            gain = jnp.where(sub == s, -gains[0, 2 * s + half], gain)

        def shade(j, carry, half=half, gain=gain):
            lanes = pl.ds(pl.multiple_of(j * 128, 128), 128)
            live = lives[j, pl.ds(half, 8, stride=2), :]
            tau = jnp.zeros((8, 128), F32)
            through = jnp.ones((8, 128), F32)
            sums = [jnp.zeros((8, 128), F32)] * 3
            for z in range(32):
                x = dens[half, z * 8 : z * 8 + 8, lanes]
                soft = jnp.log(1.0 + jnp.exp(x))
                tau = tau + jnp.where(live > z, soft * gain, 0.0)
                after = jnp.exp(tau)
                glow = through - after
                through = after
                for k in range(3):
                    sums[k] = sums[k] + glow * jnp.tanh(x * slopes[k])
            solid = 1.0 - through
            for k in range(3):
                shaded[k, j] = 0.5 * (solid + sums[k])
            shaded[3, j] = through
            return carry

        lax.fori_loop(0, 8, shade, 0)

        source = (lane % 8) * 16 + (lane // 8 % 8) * 2 + lane // 64
        for k in range(4):
            parts = [
                jnp.take_along_axis(shaded[k, j], source, axis=1, mode="promise_in_bounds")
                for j in range(8)
            ]
            for bit in range(3):
                step = 1 << bit
                upper = (lane // (8 * step)) % 2 == 1
                for j in range(8):
                    if j & step:
                        continue
                    a, b = parts[j], parts[j + step]
                    parts[j] = jnp.where(upper, pltpu.roll(b, 8 * step, 1), a)
                    parts[j + step] = jnp.where(upper, b, pltpu.roll(a, 128 - 8 * step, 1))
            for g in range(8):
                sends[half, g, k] = parts[g]

        for hop in (4, 3, 5, 2, 6, 1, 7):
            to = lax.rem(chip + hop, chips)
            copy = pltpu.make_async_remote_copy(
                src_ref=sends.at[half, to], dst_ref=boxes.at[me],
                send_sem=send_sem.at[half, hop], recv_sem=box_sem.at[me],
                device_id={"depth": 2 * to + half}, device_id_type=MESH,
            )
            copy.start()
            sends_started.append(copy)

        @pl.when(core == half)
        def _(half=half):
            pltpu.make_async_copy(sends.at[half, chip], boxes.at[me], box_sem.at[me]).start()

        @pl.when(core != half)
        def _(half=half):
            pltpu.make_async_remote_copy(
                src_ref=sends.at[half, chip], dst_ref=boxes.at[me],
                send_sem=send_sem.at[0, 0], recv_sem=box_sem.at[me],
                device_id={"depth": 2 * chip + half}, device_id_type=MESH,
            ).start()

        if half == 0:
            for hop in range(1, y_count):
                there = lax.rem(my_y + y_count - hop, y_count)
                pltpu.make_async_copy(row_got.at[there], row_got.at[there], row_box.at[there]).wait()
            block = jnp.zeros((8, 128), I32)
            for y in range(y_count):
                block = jnp.where(sub == y, row_got[y], block)
            block_send[...] = block
            block_got[my_x] = block
            for hop in range(1, x_count):
                there = lax.rem(my_x + hop, x_count) * y_count + my_y
                copy = pltpu.make_async_remote_copy(
                    src_ref=block_send, dst_ref=block_got.at[my_x],
                    send_sem=block_sems.at[hop], recv_sem=block_box.at[my_x],
                    device_id={"tile": there}, device_id_type=MESH,
                )
                copy.start()
                block_copies.append(copy)

    for hop in range(1, x_count):
        there = lax.rem(my_x + x_count - hop, x_count)
        pltpu.make_async_copy(block_got.at[there], block_got.at[there], block_box.at[there]).wait()
    total = jnp.zeros((y_count, 16), F32)
    for x in range(x_count):
        grade = block_got[x][0:y_count, 0:16]
        worth = jnp.where(grade == 2, 1.0, jnp.where(grade == 1, 0.25, 0.0625))
        total = total + jnp.where(owners[0, x * y_count : (x + 1) * y_count] == tile, worth, 0.0)
    share[...] = jnp.sum(total, keepdims=True) * (1.0 / 16.0)

    through = jnp.ones((8, 128), F32)
    colors = [jnp.zeros((8, 128), F32)] * 3
    for d in range(depth_count):
        pltpu.make_async_copy(boxes.at[d], boxes.at[d], box_sem.at[d]).wait()
        for k in range(3):
            colors[k] = colors[k] + through * boxes[d, k]
        through = through * boxes[d, 3]
    final = colors + [1.0 - through]
    for k in range(4):
        mine[k] = final[k]
    swap = pltpu.make_async_remote_copy(
        src_ref=mine, dst_ref=other, send_sem=pair_sem.at[0], recv_sem=pair_sem.at[1],
        device_id={"depth": me + 1 - 2 * core}, device_id_type=MESH,
    )
    swap.start()
    for copy in sends_started + row_copies + block_copies:
        copy.wait_send()
    pltpu.make_async_remote_copy(
        src_ref=sends.at[0, 0], dst_ref=boxes.at[me],
        send_sem=send_sem.at[0, 0], recv_sem=box_sem.at[me],
        device_id={"depth": me + 1 - 2 * core}, device_id_type=MESH,
    ).wait_send()
    swap.wait()
    keep = (lane // 64) == core
    for k in range(4):
        out[k] = jnp.where(keep, final[k], pltpu.roll(other[k], 64, 1))


def local(bricks, levels, counts, gains, ownership, tf_slope):
    depth_count = lax.axis_size("depth")
    tile_count = lax.axis_size("tile")
    y_count = min(8, tile_count)
    x_count = tile_count // y_count
    vmem = pl.BlockSpec(memory_space=pltpu.VMEM)
    smem = pl.BlockSpec(memory_space=pltpu.SMEM)
    anywhere = pl.BlockSpec(memory_space=pl.ANY)
    dma = pltpu.SemaphoreType.DMA
    composite, share = pl.pallas_call(
        functools.partial(kernel, depth_count, x_count, y_count),
        out_shape=(
            jax.ShapeDtypeStruct((4, 8, 128), F32),
            jax.ShapeDtypeStruct((1, 1), F32),
        ),
        in_specs=[anywhere, smem, anywhere, smem, vmem, smem],
        out_specs=(vmem, vmem),
        scratch_shapes=[
            pltpu.VMEM((16, 32, 1024), BF16),
            pltpu.VMEM((8, 16, 128), I32),
            pltpu.VMEM((256, 768), BF16),
            pltpu.VMEM((768, 1024), BF16),
            pltpu.VMEM((512, 1024), BF16),
            pltpu.VMEM((2, 256, 256), BF16),
            pltpu.VMEM((2, 256, 1024), F32),
            pltpu.VMEM((4, 8, 8, 128), F32),
            pltpu.VMEM((2, 8, 4, 8, 128), F32),
            pltpu.VMEM((16, 4, 8, 128), F32),
            pltpu.VMEM((4, 8, 128), F32),
            pltpu.VMEM((4, 8, 128), F32),
            pltpu.VMEM((8, 128), I32),
            pltpu.VMEM((8, 8, 128), I32),
            pltpu.VMEM((8, 128), I32),
            pltpu.VMEM((4, 8, 128), I32),
            dma((2,)),
            dma((8,)),
            dma((2, 8)),
            dma((16,)),
            dma((2,)),
            dma((8,)),
            dma((8,)),
            dma((4,)),
            dma((4,)),
        ],
        compiler_params=pltpu.CompilerParams(
            collective_id=0, has_side_effects=True, vmem_limit_bytes=40 * 1024 * 1024
        ),
        name="render",
    )(bricks, levels, counts, gains, ownership, tf_slope)
    return composite.reshape(4, 1, 1024), share


def solution(mesh):
    placed = (
        P("depth", "tile", None, None),
        P("depth", "tile"),
        P("depth", "tile", None),
        P("depth", "tile"),
        P("depth", None, None),
        P(),
    )
    return jax.shard_map(
        local,
        mesh=mesh,
        in_specs=placed,
        out_specs=(P(None, "depth", "tile"), P("depth", "tile")),
        check_vma=False,
    )
```

```python
import functools

import jax
import jax.numpy as jnp
from jax import lax
from jax.experimental import pallas as pl
from jax.experimental.pallas import tpu as pltpu
from jax.sharding import PartitionSpec as P

F32 = jnp.float32
BF16 = jnp.bfloat16
I32 = jnp.int32
MESH = pl.DeviceIdType.MESH


def tent(at, cell):
    return jnp.maximum(0.0, 1.0 - jnp.abs(at - cell))


def coarse_at(fine, side):
    return jnp.clip((fine + 0.5) * (side / 32.0) - 0.5, 0.0, side - 1.0)


def fill_plane_maps(maps):
    lane = lax.broadcasted_iota(I32, (8, 1024), 1)
    y_of = (lane // 32).astype(F32)
    x_of = lax.broadcasted_iota(I32, (32, 128), 1) % 32
    e_of = lax.broadcasted_iota(I32, (32, 128), 0).astype(F32)
    for first, side in ((0, 8), (256, 16)):
        along_x = tent(coarse_at(x_of.astype(F32), side), e_of)
        along_x = jnp.concatenate([along_x] * 8, axis=1)
        y_at = coarse_at(y_of, side)

        def one(c, carry, first=first, along_x=along_x, y_at=y_at):
            along_y = tent(y_at, c.astype(F32))
            both = along_x * jnp.concatenate([along_y] * 4, axis=0)
            maps[pl.ds(pl.multiple_of(first + c * 32, 32), 32), :] = both.astype(BF16)
            return carry

        lax.fori_loop(0, side, one, 0)


def brick_of(slot):
    half, place = slot // 8, slot % 8
    return 8 * half + 2 * (place % 4) + place // 4


def depth_map(levels, half):
    lane = lax.broadcasted_iota(I32, (1, 256), 1)
    slot = lane // 32
    grade = jnp.zeros((1, 256), I32)
    for s in range(8):
        grade = jnp.where(slot == s, levels[0, brick_of(8 * half + s)], grade)
    side = jnp.where(grade == 2, 32.0, jnp.where(grade == 1, 16.0, 8.0))
    cell = lane % 32
    cell = jnp.where(grade == 2, cell, cell % 16).astype(F32)
    row = lax.broadcasted_iota(I32, (256, 256), 0)
    z_of = (row // 8).astype(F32)
    at = jnp.minimum(jnp.maximum((z_of + 0.5) * (side / 32.0) - 0.5, 0.0), side - 1.0)
    same = (row % 8) == (lax.broadcasted_iota(I32, (256, 256), 1) // 32)
    return jnp.where(same, tent(at, cell), 0.0).astype(BF16)


def kernel(
    depth_count, x_count, y_count,
    bricks, levels_in, counts, gains_in, owners_in, slope_in,
    out, share,
    levels, gains, slope, owners,
    raw, lives, masked, maps, cells, zmaps, dens, shaded, sends, boxes,
    col_send, col_got, block_send, block_got,
    small_sem, brick_sem, live_sem, send_sem, box_sem, col_sems, col_box, block_sems, block_box,
):
    me = lax.axis_index("depth")
    tile = lax.axis_index("tile")
    my_x, my_y = tile // y_count, tile % y_count

    fetch_small = [
        pltpu.make_async_copy(there, here, small_sem.at[i])
        for i, (there, here) in enumerate(
            ((levels_in, levels), (gains_in, gains), (slope_in, slope), (owners_in.at[0], owners))
        )
    ]
    fetch_bricks = [
        pltpu.make_async_copy(bricks.at[0, pl.ds(i * 4, 4)], raw.at[pl.ds(i * 4, 4)], brick_sem.at[i])
        for i in range(4)
    ]
    fetch_lives = [
        pltpu.make_async_copy(counts.at[0, :, pl.ds(j * 128, 128)], lives.at[j], live_sem.at[j])
        for j in range(8)
    ]
    for copy in fetch_small + fetch_bricks + fetch_lives:
        copy.start()

    barrier = pltpu.get_barrier_semaphore()

    def greet_depth(hop, carry):
        pl.semaphore_signal(barrier, inc=1, device_id={"depth": lax.rem(me + hop, depth_count)}, device_id_type=MESH)
        return carry

    lax.fori_loop(1, depth_count, greet_depth, 0)
    for hop in range(1, y_count):
        there = my_x * y_count + lax.rem(my_y + hop, y_count)
        pl.semaphore_signal(barrier, inc=1, device_id={"tile": there}, device_id_type=MESH)
    for hop in range(1, x_count):
        there = lax.rem(my_x + hop, x_count) * y_count + my_y
        pl.semaphore_signal(barrier, inc=1, device_id={"tile": there}, device_id_type=MESH)

    fill_plane_maps(maps)
    for copy in fetch_small:
        copy.wait()
    for half in range(2):
        zmaps[half] = depth_map(levels, half)

    for copy in fetch_bricks:
        copy.wait()
    for slot in range(16):
        b = brick_of(slot)
        grade = levels[0, b]
        rows = pl.ds(slot * 16, 16)
        for first, width, wanted in ((0, 256, 0), (256, 512, 1)):
            keep = jnp.full((16, width), jnp.where(grade == wanted, 1.0, 0.0), F32).astype(BF16)
            masked[rows, first : first + width] = raw[b, 0:16, 0:width] * keep

    for n in range(4):
        lanes = pl.ds(n * 256, 256)
        plane = jnp.dot(masked[...], maps[:, lanes], preferred_element_type=F32)
        high = plane.astype(BF16)
        low = (plane - high.astype(F32)).astype(BF16)
        for slot in range(16):
            b = brick_of(slot)
            keep = jnp.full((16, 256), jnp.where(levels[0, b] == 2, 1.0, 0.0), F32).astype(BF16)
            here = slice(slot * 16, slot * 16 + 16)
            cells[pl.ds(slot * 32, 16), lanes] = raw[b, 0:16, lanes] * keep + high[here]
            cells[pl.ds(slot * 32 + 16, 16), lanes] = raw[b, 16:32, lanes] * keep + low[here]

    for half in range(2):
        for n in range(4):
            lanes = pl.ds(n * 256, 256)
            dens[half, :, lanes] = jnp.dot(
                zmaps[half], cells[pl.ds(half * 256, 256), lanes], preferred_element_type=F32
            )

    sub = lax.broadcasted_iota(I32, (8, 128), 0)
    lane = lax.broadcasted_iota(I32, (8, 128), 1)
    for copy in fetch_lives:
        copy.wait()
    slopes = [slope[k] * 0.5 for k in range(3)]
    copies = []

    def share_columns():
        column = lax.broadcasted_iota(I32, (16, 128), 0)
        values = jnp.zeros((16, 128), I32)
        for b in range(16):
            values = jnp.where(column == b, levels[0, b], values)
        col_send[...] = values
        col_got[my_y] = values
        for hop in range(1, y_count):
            there = my_x * y_count + lax.rem(my_y + hop, y_count)
            copy = pltpu.make_async_remote_copy(
                src_ref=col_send, dst_ref=col_got.at[my_y],
                send_sem=col_sems.at[hop], recv_sem=col_box.at[my_y],
                device_id={"tile": there}, device_id_type=MESH,
            )
            copy.start()
            copies.append(copy)

    for half in range(2):
        gain = jnp.zeros((8, 128), F32)
        for s in range(8):
            gain = jnp.where(sub == s, -gains[0, brick_of(8 * half + s)], gain)

        def shade(j, carry, half=half, gain=gain):
            lanes = pl.ds(pl.multiple_of(j * 128, 128), 128)
            live = jnp.concatenate(
                [lives[j, pl.ds(8 * half + odd, 4, stride=2), :] for odd in range(2)], axis=0
            )
            tau = jnp.zeros((8, 128), F32)
            through = jnp.ones((8, 128), F32)
            sums = [jnp.zeros((8, 128), F32)] * 3
            for z in range(32):
                x = dens[half, z * 8 : z * 8 + 8, lanes]
                soft = jnp.log(1.0 + jnp.exp(x))
                tau = tau + jnp.where(live > z, soft * gain, 0.0)
                after = jnp.exp(tau)
                glow = through - after
                through = after
                for k in range(3):
                    sums[k] = sums[k] + glow * jnp.tanh(x * slopes[k])
            solid = 1.0 - through
            for k in range(3):
                shaded[k, j] = 0.5 * (solid + sums[k])
            shaded[3, j] = through
            return carry

        lax.fori_loop(0, 8, shade, 0)

        source = (lane % 8) * 16 + (lane // 8 % 8) * 2 + lane // 64
        own_side = (lane // 64) == (sub // 4)
        for pair in range(2):
            sorted_lanes = []
            for k in (2 * pair, 2 * pair + 1):
                parts = [
                    jnp.take_along_axis(shaded[k, j], source, axis=1, mode="promise_in_bounds")
                    for j in range(8)
                ]
                for bit in range(3):
                    step = 1 << bit
                    upper = (lane // (8 * step)) % 2 == 1
                    for j in range(8):
                        if j & step:
                            continue
                        a, b = parts[j], parts[j + step]
                        parts[j] = jnp.where(upper, pltpu.roll(b, 8 * step, 1), a)
                        parts[j + step] = jnp.where(upper, b, pltpu.roll(a, 128 - 8 * step, 1))
                sorted_lanes.append(
                    [jnp.where(own_side, v, pltpu.roll(pltpu.roll(v, 64, 1), 4, 0)) for v in parts]
                )
            for g in range(8):
                first, second = sorted_lanes[0][g], sorted_lanes[1][g]
                sends[half, 2 * g, pair] = jnp.where(sub < 4, first, pltpu.roll(second, 4, 0))
                sends[half, 2 * g + 1, pair] = jnp.where(sub < 4, pltpu.roll(first, 4, 0), second)

        if half == 0:
            pl.semaphore_wait(barrier, depth_count - 1 + y_count - 1 + x_count - 1)
        for hop in (8, 7, 9, 6, 10, 5, 11, 4, 12, 3, 13, 2, 14, 1, 15):
            to = lax.rem(me + hop, depth_count)
            copy = pltpu.make_async_remote_copy(
                src_ref=sends.at[half, to], dst_ref=boxes.at[half, me],
                send_sem=send_sem.at[half, hop], recv_sem=box_sem.at[half, me],
                device_id={"depth": to}, device_id_type=MESH,
            )
            copy.start()
            copies.append(copy)
        boxes[half, me] = sends[half, me]
        if half == 0:
            share_columns()

    lane16 = lax.broadcasted_iota(I32, (16, 128), 1)
    for hop in range(1, y_count):
        there = lax.rem(my_y + hop, y_count)
        pltpu.make_async_copy(col_got.at[there], col_got.at[there], col_box.at[there]).wait()
    block = jnp.zeros((16, 128), I32)
    for y in range(y_count):
        block = jnp.where(lane16 % y_count == y, col_got[y], block)
    block_send[...] = block
    block_got[my_x] = block
    for hop in range(1, x_count):
        there = lax.rem(my_x + hop, x_count) * y_count + my_y
        copy = pltpu.make_async_remote_copy(
            src_ref=block_send, dst_ref=block_got.at[my_x],
            send_sem=block_sems.at[hop], recv_sem=block_box.at[my_x],
            device_id={"tile": there}, device_id_type=MESH,
        )
        copy.start()
        copies.append(copy)
    for hop in range(1, x_count):
        there = lax.rem(my_x + hop, x_count)
        pltpu.make_async_copy(block_got.at[there], block_got.at[there], block_box.at[there]).wait()
    grade = jnp.zeros((16, 128), I32)
    for x in range(x_count):
        grade = jnp.where(lane16 // y_count == x, block_got[x], grade)
    grade = grade[:, 0 : x_count * y_count]
    worth = jnp.where(grade == 2, 1.0, jnp.where(grade == 1, 0.25, 0.0625))
    share[...] = jnp.sum(jnp.where(owners[...] == tile, worth, 0.0), keepdims=True) * (1.0 / 16.0)

    through = []
    colors = []
    for half in range(2):
        for hop in range(1, depth_count):
            frm = lax.rem(me + hop, depth_count)
            pltpu.make_async_copy(boxes.at[half, frm], boxes.at[half, frm], box_sem.at[half, frm]).wait()
        ahead = jnp.ones((8, 128), F32)
        sums = [jnp.zeros((8, 128), F32)] * 2
        for d in range(depth_count):
            first, second = boxes[half, d, 0], boxes[half, d, 1]
            sums = [sums[0] + ahead * first, sums[1] + ahead * second]
            ahead = ahead * jnp.where(sub < 4, pltpu.roll(second, 4, 0), second)
        through.append(ahead)
        colors.append(sums)
    low = sub < 4
    out[0] = jnp.where(low, colors[0][0], pltpu.roll(colors[1][0], 4, 0))
    out[1] = jnp.where(low, pltpu.roll(colors[0][0], 4, 0), colors[1][0])
    out[2] = jnp.where(low, colors[0][1], pltpu.roll(colors[1][1], 4, 0))
    out[3] = 1.0 - jnp.where(low, through[0], through[1])
    for copy in copies:
        copy.wait_send()


def local(bricks, levels, counts, gains, ownership, tf_slope):
    depth_count = lax.axis_size("depth")
    tile_count = lax.axis_size("tile")
    y_count = min(8, tile_count)
    x_count = tile_count // y_count
    vmem = pl.BlockSpec(memory_space=pltpu.VMEM)
    anywhere = pl.BlockSpec(memory_space=pl.ANY)
    dma = pltpu.SemaphoreType.DMA
    composite, share = pl.pallas_call(
        functools.partial(kernel, depth_count, x_count, y_count),
        out_shape=(
            jax.ShapeDtypeStruct((4, 8, 128), F32),
            jax.ShapeDtypeStruct((1, 1), F32),
        ),
        in_specs=[anywhere] * 6,
        out_specs=(vmem, vmem),
        scratch_shapes=[
            pltpu.SMEM((1, 16), I32),
            pltpu.SMEM((1, 16), F32),
            pltpu.SMEM((3,), F32),
            pltpu.VMEM((16, tile_count), I32),
            pltpu.VMEM((16, 32, 1024), BF16),
            pltpu.VMEM((8, 16, 128), I32),
            pltpu.VMEM((256, 768), BF16),
            pltpu.VMEM((768, 1024), BF16),
            pltpu.VMEM((512, 1024), BF16),
            pltpu.VMEM((2, 256, 256), BF16),
            pltpu.VMEM((2, 256, 1024), F32),
            pltpu.VMEM((4, 8, 8, 128), F32),
            pltpu.VMEM((2, 16, 2, 8, 128), F32),
            pltpu.VMEM((2, 16, 2, 8, 128), F32),
            pltpu.VMEM((16, 128), I32),
            pltpu.VMEM((8, 16, 128), I32),
            pltpu.VMEM((16, 128), I32),
            pltpu.VMEM((4, 16, 128), I32),
            dma((4,)),
            dma((4,)),
            dma((8,)),
            dma((2, 16)),
            dma((2, 16)),
            dma((8,)),
            dma((8,)),
            dma((4,)),
            dma((4,)),
        ],
        compiler_params=pltpu.CompilerParams(
            collective_id=0, has_side_effects=True, vmem_limit_bytes=60 * 1024 * 1024
        ),
        name="render",
    )(bricks, levels, counts, gains, jnp.swapaxes(ownership, 1, 2), tf_slope)
    return composite.reshape(4, 1, 1024), share


def solution(mesh):
    placed = (
        P("depth", "tile", None, None),
        P("depth", "tile"),
        P("depth", "tile", None),
        P("depth", "tile"),
        P("depth", None, None),
        P(),
    )
    return jax.shard_map(
        local,
        mesh=mesh,
        in_specs=placed,
        out_specs=(P(None, "depth", "tile"), P("depth", "tile")),
        check_vma=False,
    )
```

```python
import functools

import jax
import jax.numpy as jnp
from jax import lax
from jax.experimental import pallas as pl
from jax.experimental.pallas import tpu as pltpu
from jax.sharding import PartitionSpec as P

F32 = jnp.float32
BF16 = jnp.bfloat16
I32 = jnp.int32
MESH = pl.DeviceIdType.MESH
CODE_FLOOR = -20.75
CODE_SCALE = 65535.0 / 23.75


def tent(at, cell):
    return jnp.maximum(0.0, 1.0 - jnp.abs(at - cell))


def coarse_at(fine, side):
    return jnp.clip((fine + 0.5) * (side / 32.0) - 0.5, 0.0, side - 1.0)


def fill_plane_maps(maps):
    lane = lax.broadcasted_iota(I32, (8, 1024), 1)
    y_of = (lane // 32).astype(F32)
    x_of = lax.broadcasted_iota(I32, (32, 128), 1) % 32
    e_of = lax.broadcasted_iota(I32, (32, 128), 0).astype(F32)
    for first, side in ((0, 8), (256, 16)):
        along_x = tent(coarse_at(x_of.astype(F32), side), e_of)
        along_x = jnp.concatenate([along_x] * 8, axis=1)
        y_at = coarse_at(y_of, side)

        def one(c, carry, first=first, along_x=along_x, y_at=y_at):
            along_y = tent(y_at, c.astype(F32))
            both = along_x * jnp.concatenate([along_y] * 4, axis=0)
            maps[pl.ds(pl.multiple_of(first + c * 32, 32), 32), :] = both.astype(BF16)
            return carry

        lax.fori_loop(0, side, one, 0)


def brick_of(slot):
    half, place = slot // 8, slot % 8
    return 8 * half + 2 * (place % 4) + place // 4


def depth_map(levels, half):
    lane = lax.broadcasted_iota(I32, (1, 256), 1)
    slot = lane // 32
    grade = jnp.zeros((1, 256), I32)
    for s in range(8):
        grade = jnp.where(slot == s, levels[0, brick_of(8 * half + s)], grade)
    side = jnp.where(grade == 2, 32.0, jnp.where(grade == 1, 16.0, 8.0))
    cell = lane % 32
    cell = jnp.where(grade == 2, cell, cell % 16).astype(F32)
    row = lax.broadcasted_iota(I32, (256, 256), 0)
    z_of = (row // 8).astype(F32)
    at = jnp.minimum(jnp.maximum((z_of + 0.5) * (side / 32.0) - 0.5, 0.0), side - 1.0)
    same = (row % 8) == (lax.broadcasted_iota(I32, (256, 256), 1) // 32)
    return jnp.where(same, tent(at, cell), 0.0).astype(BF16)


def encode(tau, solid, sums):
    scale = 32767.5 / jnp.maximum(solid, 1e-12)
    codes = [
        jnp.clip(sums[k] * scale + 32768.0, 0.0, 65535.0).astype(I32) for k in range(3)
    ]
    depth = jnp.log2(jnp.maximum(-tau, 1e-12))
    codes.append(jnp.clip((depth - CODE_FLOOR) * CODE_SCALE + 0.5, 0.0, 65535.0).astype(I32))
    return codes[0] | (codes[1] << 16), codes[2] | (codes[3] << 16)


def kernel(
    depth_count, x_count, y_count,
    bricks, levels_in, counts, gains_in, owners_in, slope_in,
    boxes, share,
    levels, gains, slope, owners,
    raw, lives, masked, maps, cells, zmaps, dens, shaded, sends,
    row_send, row_got, near_send, near_got, far_send, far_got,
    small_sem, brick_sem, live_sem, send_sem, box_sem,
    row_sems, row_box, near_sems, near_box, far_sems, far_box,
):
    me = lax.axis_index("depth")
    tile = lax.axis_index("tile")
    my_x, my_y = tile // y_count, tile % y_count
    near = sorted({hop % y_count for hop in (1, 2, -1, -2)} - {0})
    far = sorted({hop % y_count for hop in (2, -2)} - {0})

    fetch_small = [
        pltpu.make_async_copy(there, here, small_sem.at[i])
        for i, (there, here) in enumerate(
            ((levels_in, levels), (gains_in, gains), (slope_in, slope), (owners_in.at[0], owners))
        )
    ]
    fetch_bricks = [
        pltpu.make_async_copy(bricks.at[0, pl.ds(i * 4, 4)], raw.at[pl.ds(i * 4, 4)], brick_sem.at[i])
        for i in range(4)
    ]
    fetch_lives = [
        pltpu.make_async_copy(counts.at[0, :, pl.ds(j * 128, 128)], lives.at[j], live_sem.at[j])
        for j in range(8)
    ]
    for copy in fetch_small + fetch_bricks + fetch_lives:
        copy.start()

    barrier = pltpu.get_barrier_semaphore()

    def greet_depth(hop, carry):
        pl.semaphore_signal(barrier, inc=1, device_id={"depth": lax.rem(me + hop, depth_count)}, device_id_type=MESH)
        return carry

    lax.fori_loop(1, depth_count, greet_depth, 0)
    for hop in near:
        there = my_x * y_count + lax.rem(my_y + hop, y_count)
        pl.semaphore_signal(barrier, inc=1, device_id={"tile": there}, device_id_type=MESH)
    for hop in range(1, x_count):
        there = lax.rem(my_x + hop, x_count) * y_count + my_y
        pl.semaphore_signal(barrier, inc=1, device_id={"tile": there}, device_id_type=MESH)

    fill_plane_maps(maps)
    for copy in fetch_small:
        copy.wait()
    for half in range(2):
        zmaps[half] = depth_map(levels, half)

    for copy in fetch_bricks:
        copy.wait()
    for slot in range(16):
        b = brick_of(slot)
        grade = levels[0, b]
        rows = pl.ds(slot * 16, 16)
        for first, width, wanted in ((0, 256, 0), (256, 512, 1)):
            keep = jnp.full((16, width), jnp.where(grade == wanted, 1.0, 0.0), F32).astype(BF16)
            masked[rows, first : first + width] = raw[b, 0:16, 0:width] * keep

    for n in range(4):
        lanes = pl.ds(n * 256, 256)
        plane = jnp.dot(masked[...], maps[:, lanes], preferred_element_type=F32)
        high = plane.astype(BF16)
        low = (plane - high.astype(F32)).astype(BF16)
        for slot in range(16):
            b = brick_of(slot)
            keep = jnp.full((16, 256), jnp.where(levels[0, b] == 2, 1.0, 0.0), F32).astype(BF16)
            here = slice(slot * 16, slot * 16 + 16)
            cells[pl.ds(slot * 32, 16), lanes] = raw[b, 0:16, lanes] * keep + high[here]
            cells[pl.ds(slot * 32 + 16, 16), lanes] = raw[b, 16:32, lanes] * keep + low[here]

    for half in range(2):
        for n in range(4):
            lanes = pl.ds(n * 256, 256)
            dens[half, :, lanes] = jnp.dot(
                zmaps[half], cells[pl.ds(half * 256, 256), lanes], preferred_element_type=F32
            )

    sub = lax.broadcasted_iota(I32, (8, 128), 0)
    lane = lax.broadcasted_iota(I32, (8, 128), 1)
    for copy in fetch_lives:
        copy.wait()
    slopes = [slope[k] * 0.5 for k in range(3)]
    copies = []

    def tell(source, target, hops, along_x, sends_sem, gets_sem):
        for i, hop in enumerate(hops):
            if along_x:
                there = lax.rem(my_x + hop, x_count) * y_count + my_y
            else:
                there = my_x * y_count + lax.rem(my_y + hop, y_count)
            copy = pltpu.make_async_remote_copy(
                src_ref=source, dst_ref=target.at[i],
                send_sem=sends_sem.at[i], recv_sem=gets_sem.at[i],
                device_id={"tile": there}, device_id_type=MESH,
            )
            copy.start()
            copies.append(copy)

    def hear(target, hops, gets_sem):
        for i in range(len(hops)):
            pltpu.make_async_copy(target.at[i], target.at[i], gets_sem.at[i]).wait()

    place = lax.broadcasted_iota(I32, (16, 128), 1)

    for half in range(2):
        gain = jnp.zeros((8, 128), F32)
        for s in range(8):
            gain = jnp.where(sub == s, -gains[0, brick_of(8 * half + s)], gain)

        def shade(j, carry, half=half, gain=gain):
            lanes = pl.ds(pl.multiple_of(j * 128, 128), 128)
            live = jnp.concatenate(
                [lives[j, pl.ds(8 * half + odd, 4, stride=2), :] for odd in range(2)], axis=0
            )
            tau = jnp.zeros((8, 128), F32)
            through = jnp.ones((8, 128), F32)
            sums = [jnp.zeros((8, 128), F32)] * 3
            for z in range(32):
                x = dens[half, z * 8 : z * 8 + 8, lanes]
                soft = jnp.log(1.0 + jnp.exp(x))
                tau = tau + jnp.where(live > z, soft * gain, 0.0)
                after = jnp.exp(tau)
                glow = through - after
                through = after
                for k in range(3):
                    sums[k] = sums[k] + glow * jnp.tanh(x * slopes[k])
            shaded[0, j], shaded[1, j] = encode(tau, 1.0 - through, sums)
            return carry

        lax.fori_loop(0, 8, shade, 0)

        source = (lane % 8) * 16 + (lane // 8 % 8) * 2 + lane // 64
        own_side = (lane // 64) == (sub // 4)
        sorted_lanes = []
        for k in range(2):
            parts = [
                jnp.take_along_axis(shaded[k, j], source, axis=1, mode="promise_in_bounds")
                for j in range(8)
            ]
            for bit in range(3):
                step = 1 << bit
                upper = (lane // (8 * step)) % 2 == 1
                for j in range(8):
                    if j & step:
                        continue
                    a, b = parts[j], parts[j + step]
                    parts[j] = jnp.where(upper, pltpu.roll(b, 8 * step, 1), a)
                    parts[j + step] = jnp.where(upper, b, pltpu.roll(a, 128 - 8 * step, 1))
            sorted_lanes.append(
                [jnp.where(own_side, v, pltpu.roll(pltpu.roll(v, 64, 1), 4, 0)) for v in parts]
            )
        for g in range(8):
            first, second = sorted_lanes[0][g], sorted_lanes[1][g]
            sends[half, 2 * g] = jnp.where(sub < 4, first, pltpu.roll(second, 4, 0))
            sends[half, 2 * g + 1] = jnp.where(sub < 4, pltpu.roll(first, 4, 0), second)

        if half == 0:
            pl.semaphore_wait(barrier, depth_count - 1 + len(near) + x_count - 1)
        for hop in (8, 7, 9, 6, 10, 5, 11, 4, 12, 3, 13, 2, 14, 1, 15):
            to = lax.rem(me + hop, depth_count)
            copy = pltpu.make_async_remote_copy(
                src_ref=sends.at[half, to], dst_ref=boxes.at[half, me],
                send_sem=send_sem.at[half, hop], recv_sem=box_sem.at[half, me],
                device_id={"depth": to}, device_id_type=MESH,
            )
            copy.start()
            copies.append(copy)
        boxes[half, me] = sends[half, me]
        if half == 0:
            column = lax.broadcasted_iota(I32, (16, 128), 0)
            table = jnp.zeros((16, 128), I32)
            for b in range(16):
                table = jnp.where(column == b, levels[0, b], table)
            row_send[...] = table
            tell(row_send, row_got, range(1, x_count), True, row_sems, row_box)

    hear(row_got, range(1, x_count), row_box)
    for hop in range(1, x_count):
        at = lax.rem(my_x + x_count - hop, x_count)
        table = jnp.where(place // y_count == at, row_got[hop - 1], table)
    near_send[...] = table
    tell(near_send, near_got, near, False, near_sems, near_box)
    hear(near_got, near, near_box)
    for i, hop in enumerate(near):
        at = lax.rem(my_y + y_count - hop, y_count)
        table = jnp.where(place % y_count == at, near_got[i], table)
    far_send[...] = table
    tell(far_send, far_got, far, False, far_sems, far_box)
    hear(far_got, far, far_box)
    known = sorted({(-hop) % y_count for hop in near} | {0})
    for i, hop in enumerate(far):
        for step in sorted({(k - hop) % y_count for k in known} - set(known)):
            at = lax.rem(my_y + step, y_count)
            table = jnp.where(place % y_count == at, far_got[i], table)
    grade = table[:, 0 : x_count * y_count]
    worth = jnp.where(grade == 2, 1.0, jnp.where(grade == 1, 0.25, 0.0625))
    share[...] = jnp.sum(jnp.where(owners[...] == tile, worth, 0.0), keepdims=True) * (1.0 / 16.0)

    for half in range(2):
        for hop in range(1, depth_count):
            frm = lax.rem(me + hop, depth_count)
            pltpu.make_async_copy(boxes.at[half, frm], boxes.at[half, frm], box_sem.at[half, frm]).wait()
    for copy in copies:
        copy.wait_send()


def composite_kernel(depth_count, boxes, share_in, out, share):
    low = lax.broadcasted_iota(I32, (8, 128), 0) < 4
    passed, even, odd = [], [], []
    for half in range(2):
        ahead = jnp.ones((8, 128), F32)
        first = jnp.zeros((8, 128), F32)
        second = jnp.zeros((8, 128), F32)
        for d in range(depth_count):
            word = boxes[half, d]
            bottom = (word & 65535).astype(F32)
            top = lax.shift_right_logical(word, 16).astype(F32)
            code = jnp.where(low, pltpu.roll(top, 4, 0), top)
            through = jnp.exp(-jnp.exp2(code * (1.0 / CODE_SCALE) + CODE_FLOOR))
            weight = ahead * (1.0 - through)
            first = first + weight * bottom
            second = second + weight * top
            ahead = ahead * through
        passed.append(ahead)
        even.append(first * (1.0 / 65535.0))
        odd.append(second * (1.0 / 65535.0))
    out[0] = jnp.where(low, even[0], pltpu.roll(even[1], 4, 0))
    out[1] = jnp.where(low, odd[0], pltpu.roll(odd[1], 4, 0))
    out[2] = jnp.where(low, pltpu.roll(even[0], 4, 0), even[1])
    out[3] = 1.0 - jnp.where(low, passed[0], passed[1])
    share[...] = share_in[...]


def local(bricks, levels, counts, gains, ownership, tf_slope):
    depth_count = lax.axis_size("depth")
    tile_count = lax.axis_size("tile")
    y_count = min(8, tile_count)
    x_count = tile_count // y_count
    vmem = pl.BlockSpec(memory_space=pltpu.VMEM)
    anywhere = pl.BlockSpec(memory_space=pltpu.HBM)
    dma = pltpu.SemaphoreType.DMA
    boxes, share = pl.pallas_call(
        functools.partial(kernel, depth_count, x_count, y_count),
        out_shape=(
            pltpu.VMEM((2, 16, 8, 128), I32),
            pltpu.VMEM((1, 1), F32),
        ),
        in_specs=[anywhere] * 6,
        out_specs=(vmem, vmem),
        scratch_shapes=[
            pltpu.SMEM((1, 16), I32),
            pltpu.SMEM((1, 16), F32),
            pltpu.SMEM((3,), F32),
            pltpu.VMEM((16, tile_count), I32),
            pltpu.VMEM((16, 32, 1024), BF16),
            pltpu.VMEM((8, 16, 128), I32),
            pltpu.VMEM((256, 768), BF16),
            pltpu.VMEM((768, 1024), BF16),
            pltpu.VMEM((512, 1024), BF16),
            pltpu.VMEM((2, 256, 256), BF16),
            pltpu.VMEM((2, 256, 1024), F32),
            pltpu.VMEM((2, 8, 8, 128), I32),
            pltpu.VMEM((2, 16, 8, 128), I32),
            pltpu.VMEM((16, 128), I32),
            pltpu.VMEM((3, 16, 128), I32),
            pltpu.VMEM((16, 128), I32),
            pltpu.VMEM((4, 16, 128), I32),
            pltpu.VMEM((16, 128), I32),
            pltpu.VMEM((2, 16, 128), I32),
            dma((4,)),
            dma((4,)),
            dma((8,)),
            dma((2, 16)),
            dma((2, 16)),
            dma((3,)),
            dma((3,)),
            dma((4,)),
            dma((4,)),
            dma((2,)),
            dma((2,)),
        ],
        compiler_params=pltpu.CompilerParams(
            collective_id=0, has_side_effects=True, vmem_limit_bytes=56000 * 1024
        ),
        name="render",
    )(bricks, levels, counts, gains, jnp.swapaxes(ownership, 1, 2), tf_slope)
    composite, share = pl.pallas_call(
        functools.partial(composite_kernel, depth_count),
        out_shape=(
            jax.ShapeDtypeStruct((4, 8, 128), F32),
            jax.ShapeDtypeStruct((1, 1), F32),
        ),
        in_specs=[vmem, vmem],
        out_specs=(vmem, vmem),
        compiler_params=pltpu.CompilerParams(vmem_limit_bytes=4 * 1024 * 1024),
        name="composite",
    )(boxes, share)
    return composite.reshape(4, 1, 1024), share


def solution(mesh):
    placed = (
        P("depth", "tile", None, None),
        P("depth", "tile"),
        P("depth", "tile", None),
        P("depth", "tile"),
        P("depth", None, None),
        P(),
    )
    return jax.shard_map(
        local,
        mesh=mesh,
        in_specs=placed,
        out_specs=(P(None, "depth", "tile"), P("depth", "tile")),
        check_vma=False,
    )
```

```python
import functools

import jax
import jax.numpy as jnp
from jax import lax
from jax.experimental import pallas as pl
from jax.experimental.pallas import tpu as pltpu
from jax.sharding import PartitionSpec as P

F32 = jnp.float32
BF16 = jnp.bfloat16
I32 = jnp.int32
MESH = pl.DeviceIdType.MESH
CODE_FLOOR = -20.75
CODE_SCALE = 65535.0 / 23.75


def tent(at, cell):
    return jnp.maximum(0.0, 1.0 - jnp.abs(at - cell))


def coarse_at(fine, side):
    return jnp.clip((fine + 0.5) * (side / 32.0) - 0.5, 0.0, side - 1.0)


def fill_plane_maps(maps):
    lane = lax.broadcasted_iota(I32, (8, 1024), 1)
    y_of = (lane // 32).astype(F32)
    x_of = lax.broadcasted_iota(I32, (32, 128), 1) % 32
    e_of = lax.broadcasted_iota(I32, (32, 128), 0).astype(F32)
    for first, side in ((0, 8), (256, 16)):
        along_x = tent(coarse_at(x_of.astype(F32), side), e_of)
        along_x = jnp.concatenate([along_x] * 8, axis=1)
        y_at = coarse_at(y_of, side)

        def one(c, carry, first=first, along_x=along_x, y_at=y_at):
            along_y = tent(y_at, c.astype(F32))
            both = along_x * jnp.concatenate([along_y] * 4, axis=0)
            maps[pl.ds(pl.multiple_of(first + c * 32, 32), 32), :] = both.astype(BF16)
            return carry

        lax.fori_loop(0, side, one, 0)


def brick_of(slot):
    half, place = slot // 8, slot % 8
    return 8 * half + 2 * (place % 4) + place // 4


def depth_map(levels, half):
    lane = lax.broadcasted_iota(I32, (1, 256), 1)
    slot = lane // 32
    grade = jnp.zeros((1, 256), I32)
    for s in range(8):
        grade = jnp.where(slot == s, levels[0, brick_of(8 * half + s)], grade)
    side = jnp.where(grade == 2, 32.0, jnp.where(grade == 1, 16.0, 8.0))
    cell = lane % 32
    cell = jnp.where(grade == 2, cell, cell % 16).astype(F32)
    row = lax.broadcasted_iota(I32, (256, 256), 0)
    z_of = (row // 8).astype(F32)
    at = jnp.minimum(jnp.maximum((z_of + 0.5) * (side / 32.0) - 0.5, 0.0), side - 1.0)
    same = (row % 8) == (lax.broadcasted_iota(I32, (256, 256), 1) // 32)
    return jnp.where(same, tent(at, cell), 0.0).astype(BF16)


def encode(tau, solid, sums):
    scale = 32767.5 / jnp.maximum(solid, 1e-12)
    codes = [
        jnp.clip(sums[k] * scale + 32768.0, 0.0, 65535.0).astype(I32) for k in range(3)
    ]
    depth = jnp.log2(jnp.maximum(-tau, 1e-12))
    codes.append(jnp.clip((depth - CODE_FLOOR) * CODE_SCALE + 0.5, 0.0, 65535.0).astype(I32))
    return codes[0] | (codes[1] << 16), codes[2] | (codes[3] << 16)


def swapped(place):
    return place + 1 - 2 * (place % 2)


def wait_for(semaphore, count):
    @pl.when(count > 0)
    def _():
        pl.semaphore_wait(semaphore, count)


def y_order(y, count):
    back = count - y
    return jnp.where(y <= back, jnp.maximum(2 * y - 1, 0), 2 * back)


def y_at(order, count):
    return jnp.where(order % 2 == 1, (order + 1) // 2, (count - order // 2) % count)


def kernel(
    depth_count, x_count, y_count,
    bricks, levels_in, counts, gains_in, owners_in, slope_in,
    boxes, share,
    levels, gains, slope, owners,
    raw, lives, masked, maps, cells, zmaps, dens, shaded, sends,
    row_send, block_send, x_rows, y_rows,
    small_sem, brick_sem, live_sem, send_sem, box_sem,
    row_sem, row_box, depth_ready, x_ready, y_ready,
):
    me = lax.axis_index("depth")
    tile = lax.axis_index("tile")
    tile_count = x_count * y_count
    my_x, my_y = tile // y_count, tile % y_count

    fetch_small = [
        pltpu.make_async_copy(there, here, small_sem.at[i])
        for i, (there, here) in enumerate(
            ((levels_in, levels), (gains_in, gains), (slope_in, slope), (owners_in.at[0], owners))
        )
    ]
    fetch_bricks = [
        pltpu.make_async_copy(bricks.at[0, pl.ds(i * 4, 4)], raw.at[pl.ds(i * 4, 4)], brick_sem.at[i])
        for i in range(4)
    ]
    fetch_lives = [
        pltpu.make_async_copy(counts.at[0, :, pl.ds(j * 128, 128)], lives.at[j], live_sem.at[j])
        for j in range(8)
    ]
    for copy in fetch_bricks + fetch_small + fetch_lives:
        copy.start()

    barrier = pltpu.get_barrier_semaphore()
    order = swapped(me)

    def greet(peer, carry):
        pl.semaphore_signal(barrier, inc=1, device_id={"depth": swapped(peer)}, device_id_type=MESH)
        return carry

    lax.fori_loop(order + 1, depth_count, greet, 0)
    my_order = y_order(my_y, y_count)

    def at_x(x):
        return {"tile": x * y_count + my_y}

    def at_y(place):
        return {"tile": my_x * y_count + y_at(place, y_count)}

    def signal(semaphore, device):
        def one(peer, carry):
            pl.semaphore_signal(semaphore, inc=1, device_id=device(peer), device_id_type=MESH)
            return carry

        return one

    lax.fori_loop(my_x + 1, x_count, signal(barrier, at_x), 0)
    lax.fori_loop(my_order + 1, y_count, signal(barrier, at_y), 0)

    fill_plane_maps(maps)
    for copy in fetch_small:
        copy.wait()
    for half in range(2):
        zmaps[half] = depth_map(levels, half)

    for copy in fetch_bricks:
        copy.wait()
    for slot in range(16):
        b = brick_of(slot)
        grade = levels[0, b]
        rows = pl.ds(slot * 16, 16)
        for first, width, wanted in ((0, 256, 0), (256, 512, 1)):
            keep = jnp.full((16, width), jnp.where(grade == wanted, 1.0, 0.0), F32).astype(BF16)
            masked[rows, first : first + width] = raw[b, 0:16, 0:width] * keep

    for n in range(4):
        lanes = pl.ds(n * 256, 256)
        plane = jnp.dot(masked[...], maps[:, lanes], preferred_element_type=F32)
        high = plane.astype(BF16)
        low = (plane - high.astype(F32)).astype(BF16)
        for slot in range(16):
            b = brick_of(slot)
            keep = jnp.full((16, 256), jnp.where(levels[0, b] == 2, 1.0, 0.0), F32).astype(BF16)
            here = slice(slot * 16, slot * 16 + 16)
            cells[pl.ds(slot * 32, 16), lanes] = raw[b, 0:16, lanes] * keep + high[here]
            cells[pl.ds(slot * 32 + 16, 16), lanes] = raw[b, 16:32, lanes] * keep + low[here]

    for half in range(2):
        for n in range(4):
            lanes = pl.ds(n * 256, 256)
            dens[half, :, lanes] = jnp.dot(
                zmaps[half], cells[pl.ds(half * 256, 256), lanes], preferred_element_type=F32
            )

    sub = lax.broadcasted_iota(I32, (8, 128), 0)
    lane = lax.broadcasted_iota(I32, (8, 128), 1)
    for copy in fetch_lives:
        copy.wait()
    slopes = [slope[k] * 0.5 for k in range(3)]

    def pixels(half, to):
        return pltpu.make_async_remote_copy(
            src_ref=sends.at[half, to], dst_ref=boxes.at[half, me],
            send_sem=send_sem.at[half], recv_sem=box_sem.at[half],
            device_id={"depth": to}, device_id_type=MESH,
        )

    def send(half, peer, carry):
        pixels(half, swapped(peer)).start()
        return carry

    def along_x(x):
        return pltpu.make_async_remote_copy(
            src_ref=row_send, dst_ref=x_rows.at[my_x], send_sem=row_sem.at[0], recv_sem=row_box.at[0],
            device_id=at_x(x), device_id_type=MESH,
        )

    def along_y(place):
        return pltpu.make_async_remote_copy(
            src_ref=block_send, dst_ref=y_rows.at[my_y], send_sem=row_sem.at[1], recv_sem=row_box.at[1],
            device_id=at_y(place), device_id_type=MESH,
        )

    def start(copy):
        def one(peer, carry):
            copy(peer).start()
            return carry

        return one

    def take(buffer, count, semaphore):
        if count:
            some = buffer.at[pl.ds(0, count)]
            pltpu.make_async_copy(some, some, semaphore).wait()

    packed = jnp.zeros((8, 128), I32)
    for s in range(8):
        packed = jnp.where(sub == s, levels[0, s] + 256 * levels[0, s + 8], packed)
    row_send[...] = packed
    x_rows[my_x] = packed

    for half in range(2):
        gain = jnp.zeros((8, 128), F32)
        for s in range(8):
            gain = jnp.where(sub == s, -gains[0, brick_of(8 * half + s)], gain)

        def shade(j, carry, half=half, gain=gain):
            lanes = pl.ds(pl.multiple_of(j * 128, 128), 128)
            live = jnp.concatenate(
                [lives[j, pl.ds(8 * half + odd, 4, stride=2), :] for odd in range(2)], axis=0
            )
            tau = jnp.zeros((8, 128), F32)
            through = jnp.ones((8, 128), F32)
            sums = [jnp.zeros((8, 128), F32)] * 3
            for z in range(32):
                x = dens[half, z * 8 : z * 8 + 8, lanes]
                soft = jnp.log(1.0 + jnp.exp(x))
                tau = tau + jnp.where(live > z, soft * gain, 0.0)
                after = jnp.exp(tau)
                glow = through - after
                through = after
                for k in range(3):
                    sums[k] = sums[k] + glow * jnp.tanh(x * slopes[k])
            shaded[0, j], shaded[1, j] = encode(tau, 1.0 - through, sums)
            return carry

        lax.fori_loop(0, 8, shade, 0)

        source = (lane % 8) * 16 + (lane // 8 % 8) * 2 + lane // 64
        own_side = (lane // 64) == (sub // 4)
        sorted_lanes = []
        for k in range(2):
            parts = [
                jnp.take_along_axis(shaded[k, j], source, axis=1, mode="promise_in_bounds")
                for j in range(8)
            ]
            for bit in range(3):
                step = 1 << bit
                upper = (lane // (8 * step)) % 2 == 1
                for j in range(8):
                    if j & step:
                        continue
                    a, b = parts[j], parts[j + step]
                    parts[j] = jnp.where(upper, pltpu.roll(b, 8 * step, 1), a)
                    parts[j + step] = jnp.where(upper, b, pltpu.roll(a, 128 - 8 * step, 1))
            sorted_lanes.append(
                [jnp.where(own_side, v, pltpu.roll(pltpu.roll(v, 64, 1), 4, 0)) for v in parts]
            )
        for g in range(8):
            first, second = sorted_lanes[0][g], sorted_lanes[1][g]
            sends[half, 2 * g] = jnp.where(sub < 4, first, pltpu.roll(second, 4, 0))
            sends[half, 2 * g + 1] = jnp.where(sub < 4, pltpu.roll(first, 4, 0), second)

        if half == 0:
            wait_for(barrier, order + my_x + my_order)
        lax.fori_loop(0, order, functools.partial(send, half), 0)
        boxes[half, me] = sends[half, me]
    lax.fori_loop(0, order, signal(depth_ready, lambda peer: {"depth": swapped(peer)}), 0)
    lax.fori_loop(0, my_x, signal(x_ready, at_x), 0)
    lax.fori_loop(0, my_order, signal(y_ready, at_y), 0)
    lax.fori_loop(0, my_x, start(along_x), 0)

    def serve_later():
        wait_for(depth_ready, depth_count - 1 - order)
        for half in range(2):
            lax.fori_loop(order + 1, depth_count, functools.partial(send, half), 0)

    pl.when(me >= depth_count // 2)(serve_later)

    wait_for(x_ready, x_count - 1 - my_x)
    lax.fori_loop(my_x + 1, x_count, start(along_x), 0)
    take(x_rows, x_count - 1, row_box.at[0])
    table = jnp.zeros((8, 128), I32)
    for x in range(x_count):
        table = jnp.where(lane // y_count == x, x_rows[x], table)
    block_send[...] = table
    y_rows[my_y] = table
    wait_for(y_ready, y_count - 1 - my_order)
    lax.fori_loop(0, my_order, start(along_y), 0)
    lax.fori_loop(my_order + 1, y_count, start(along_y), 0)
    take(y_rows, y_count - 1, row_box.at[1])
    for y in range(y_count):
        table = jnp.where(lane % y_count == y, y_rows[y], table)
    table = table[:, 0:tile_count]
    total = jnp.zeros((8, tile_count), F32)
    for part, grade in enumerate((table & 255, table >> 8)):
        worth = jnp.where(grade == 2, 1.0, jnp.where(grade == 1, 0.25, 0.0625))
        total = total + jnp.where(owners[8 * part : 8 * part + 8] == tile, worth, 0.0)
    share[...] = jnp.sum(total, keepdims=True) * (1.0 / 16.0)

    pl.when(me < depth_count // 2)(serve_later)

    take(x_rows, x_count - 1, row_sem.at[0])
    take(y_rows, y_count - 1, row_sem.at[1])
    for half in range(2):
        take(sends.at[half], depth_count - 1, send_sem.at[half])
    for half in range(2):
        take(boxes.at[half], depth_count - 1, box_sem.at[half])


def composite_kernel(depth_count, boxes, share_in, out, share):
    low = lax.broadcasted_iota(I32, (8, 128), 0) < 4
    passed, even, odd = [], [], []
    for half in range(2):
        ahead = jnp.ones((8, 128), F32)
        first = jnp.zeros((8, 128), F32)
        second = jnp.zeros((8, 128), F32)
        for d in range(depth_count):
            word = boxes[half, d]
            bottom = (word & 65535).astype(F32)
            top = lax.shift_right_logical(word, 16).astype(F32)
            code = jnp.where(low, pltpu.roll(top, 4, 0), top)
            through = jnp.exp(-jnp.exp2(code * (1.0 / CODE_SCALE) + CODE_FLOOR))
            weight = ahead * (1.0 - through)
            first = first + weight * bottom
            second = second + weight * top
            ahead = ahead * through
        passed.append(ahead)
        even.append(first * (1.0 / 65535.0))
        odd.append(second * (1.0 / 65535.0))
    out[0] = jnp.where(low, even[0], pltpu.roll(even[1], 4, 0))
    out[1] = jnp.where(low, odd[0], pltpu.roll(odd[1], 4, 0))
    out[2] = jnp.where(low, pltpu.roll(even[0], 4, 0), even[1])
    out[3] = 1.0 - jnp.where(low, passed[0], passed[1])
    share[...] = share_in[...]


def local(bricks, levels, counts, gains, ownership, tf_slope):
    depth_count = lax.axis_size("depth")
    tile_count = lax.axis_size("tile")
    y_count = min(8, tile_count)
    x_count = tile_count // y_count
    vmem = pl.BlockSpec(memory_space=pltpu.VMEM)
    anywhere = pl.BlockSpec(memory_space=pltpu.HBM)
    dma = pltpu.SemaphoreType.DMA
    boxes, share = pl.pallas_call(
        functools.partial(kernel, depth_count, x_count, y_count),
        out_shape=(
            pltpu.VMEM((2, 16, 8, 128), I32),
            pltpu.VMEM((1, 1), F32),
        ),
        in_specs=[anywhere] * 6,
        out_specs=(vmem, vmem),
        scratch_shapes=[
            pltpu.SMEM((1, 16), I32),
            pltpu.SMEM((1, 16), F32),
            pltpu.SMEM((3,), F32),
            pltpu.VMEM((16, tile_count), I32),
            pltpu.VMEM((16, 32, 1024), BF16),
            pltpu.VMEM((8, 16, 128), I32),
            pltpu.VMEM((256, 768), BF16),
            pltpu.VMEM((768, 1024), BF16),
            pltpu.VMEM((512, 1024), BF16),
            pltpu.VMEM((2, 256, 256), BF16),
            pltpu.VMEM((2, 256, 1024), F32),
            pltpu.VMEM((2, 8, 8, 128), I32),
            pltpu.VMEM((2, 16, 8, 128), I32),
            pltpu.VMEM((8, 128), I32),
            pltpu.VMEM((8, 128), I32),
            pltpu.VMEM((x_count, 8, 128), I32),
            pltpu.VMEM((y_count, 8, 128), I32),
            dma((4,)),
            dma((4,)),
            dma((8,)),
            dma((2,)),
            dma((2,)),
            dma((2,)),
            dma((2,)),
            pltpu.SemaphoreType.REGULAR,
            pltpu.SemaphoreType.REGULAR,
            pltpu.SemaphoreType.REGULAR,
        ],
        compiler_params=pltpu.CompilerParams(
            collective_id=0, has_side_effects=True, vmem_limit_bytes=56000 * 1024
        ),
        name="render",
    )(bricks, levels, counts, gains, jnp.swapaxes(ownership, 1, 2), tf_slope)
    composite, share = pl.pallas_call(
        functools.partial(composite_kernel, depth_count),
        out_shape=(
            jax.ShapeDtypeStruct((4, 8, 128), F32),
            jax.ShapeDtypeStruct((1, 1), F32),
        ),
        in_specs=[vmem, vmem],
        out_specs=(vmem, vmem),
        compiler_params=pltpu.CompilerParams(vmem_limit_bytes=4 * 1024 * 1024),
        name="composite",
    )(boxes, share)
    return composite.reshape(4, 1, 1024), share


def solution(mesh):
    placed = (
        P("depth", "tile", None, None),
        P("depth", "tile"),
        P("depth", "tile", None),
        P("depth", "tile"),
        P("depth", None, None),
        P(),
    )
    return jax.shard_map(
        local,
        mesh=mesh,
        in_specs=placed,
        out_specs=(P(None, "depth", "tile"), P("depth", "tile")),
        check_vma=False,
    )
```

```python
import functools

import jax
import jax.numpy as jnp
from jax import lax
from jax.experimental import pallas as pl
from jax.experimental.pallas import tpu as pltpu
from jax.sharding import PartitionSpec as P

F32 = jnp.float32
BF16 = jnp.bfloat16
I32 = jnp.int32
MESH = pl.DeviceIdType.MESH
CODE_FLOOR = -20.75
CODE_SCALE = 65535.0 / 23.75


def tent(at, cell):
    return jnp.maximum(0.0, 1.0 - jnp.abs(at - cell))


def coarse_at(fine, side):
    return jnp.clip((fine + 0.5) * (side / 32.0) - 0.5, 0.0, side - 1.0)


def fill_plane_maps(maps):
    lane = lax.broadcasted_iota(I32, (8, 1024), 1)
    y_of = (lane // 32).astype(F32)
    x_of = lax.broadcasted_iota(I32, (32, 128), 1) % 32
    e_of = lax.broadcasted_iota(I32, (32, 128), 0).astype(F32)
    for first, side in ((0, 8), (256, 16)):
        along_x = tent(coarse_at(x_of.astype(F32), side), e_of)
        along_x = jnp.concatenate([along_x] * 8, axis=1)
        y_at = coarse_at(y_of, side)

        def one(c, carry, first=first, along_x=along_x, y_at=y_at):
            along_y = tent(y_at, c.astype(F32))
            both = along_x * jnp.concatenate([along_y] * 4, axis=0)
            maps[pl.ds(pl.multiple_of(first + c * 32, 32), 32), :] = both.astype(BF16)
            return carry

        lax.fori_loop(0, side, one, 0)


def brick_of(slot):
    half, place = slot // 8, slot % 8
    return 8 * half + 2 * (place % 4) + place // 4


def depth_map(levels, half):
    lane = lax.broadcasted_iota(I32, (1, 256), 1)
    slot = lane // 32
    grade = jnp.zeros((1, 256), I32)
    for s in range(8):
        grade = jnp.where(slot == s, levels[0, brick_of(8 * half + s)], grade)
    side = jnp.where(grade == 2, 32.0, jnp.where(grade == 1, 16.0, 8.0))
    cell = lane % 32
    cell = jnp.where(grade == 2, cell, cell % 16).astype(F32)
    row = lax.broadcasted_iota(I32, (256, 256), 0)
    z_of = (row // 8).astype(F32)
    at = jnp.minimum(jnp.maximum((z_of + 0.5) * (side / 32.0) - 0.5, 0.0), side - 1.0)
    same = (row % 8) == (lax.broadcasted_iota(I32, (256, 256), 1) // 32)
    return jnp.where(same, tent(at, cell), 0.0).astype(BF16)


def encode(tau, solid, sums):
    scale = 32767.5 / jnp.maximum(solid, 1e-12)
    codes = [
        jnp.clip(sums[k] * scale + 32768.0, 0.0, 65535.0).astype(I32) for k in range(3)
    ]
    depth = jnp.log2(jnp.maximum(-tau, 1e-12))
    codes.append(jnp.clip((depth - CODE_FLOOR) * CODE_SCALE + 0.5, 0.0, 65535.0).astype(I32))
    return codes[0] | (codes[1] << 16), codes[2] | (codes[3] << 16)


def swapped(place):
    return place + 1 - 2 * (place % 2)


def wait_for(semaphore, count):
    @pl.when(count > 0)
    def _():
        pl.semaphore_wait(semaphore, count)


def y_order(y, count):
    back = count - y
    return jnp.where(y <= back, jnp.maximum(2 * y - 1, 0), 2 * back)


def y_at(order, count):
    return jnp.where(order % 2 == 1, (order + 1) // 2, (count - order // 2) % count)


def kernel(
    depth_count, x_count, y_count,
    bricks, levels_in, counts, gains_in, owners_in, slope_in,
    boxes, share,
    levels, gains, slope, owners,
    raw, lives, masked, maps, cells, zmaps, dens, shaded, sends,
    row_send, block_send, x_rows, y_rows,
    small_sem, brick_sem, live_sem, send_sem, box_sem,
    row_sem, row_box, depth_ready, x_ready, y_ready,
):
    me = lax.axis_index("depth")
    tile = lax.axis_index("tile")
    tile_count = x_count * y_count
    my_x, my_y = tile // y_count, tile % y_count

    fetch_small = [
        pltpu.make_async_copy(there, here, small_sem.at[i])
        for i, (there, here) in enumerate(
            ((levels_in, levels), (gains_in, gains), (slope_in, slope), (owners_in.at[0], owners))
        )
    ]
    fetch_bricks = [
        pltpu.make_async_copy(bricks.at[0, pl.ds(i * 4, 4)], raw.at[pl.ds(i * 4, 4)], brick_sem.at[i])
        for i in range(4)
    ]
    fetch_lives = [
        pltpu.make_async_copy(counts.at[0, :, pl.ds(j * 128, 128)], lives.at[j], live_sem.at[j])
        for j in range(8)
    ]
    for copy in fetch_bricks + fetch_small + fetch_lives:
        copy.start()

    barrier = pltpu.get_barrier_semaphore()
    order = swapped(me)

    def greet(peer, carry):
        pl.semaphore_signal(barrier, inc=1, device_id={"depth": swapped(peer)}, device_id_type=MESH)
        return carry

    lax.fori_loop(order + 1, depth_count, greet, 0)
    my_order = y_order(my_y, y_count)

    def at_x(x):
        return {"tile": x * y_count + my_y}

    def at_y(place):
        return {"tile": my_x * y_count + y_at(place, y_count)}

    def signal(semaphore, device):
        def one(peer, carry):
            pl.semaphore_signal(semaphore, inc=1, device_id=device(peer), device_id_type=MESH)
            return carry

        return one

    lax.fori_loop(my_x + 1, x_count, signal(barrier, at_x), 0)
    lax.fori_loop(my_order + 1, y_count, signal(barrier, at_y), 0)

    fill_plane_maps(maps)
    for copy in fetch_small:
        copy.wait()
    for half in range(2):
        zmaps[half] = depth_map(levels, half)

    for copy in fetch_bricks:
        copy.wait()
    for slot in range(16):
        b = brick_of(slot)
        grade = levels[0, b]
        rows = pl.ds(slot * 16, 16)
        for first, width, wanted in ((0, 256, 0), (256, 512, 1)):
            keep = jnp.full((16, width), jnp.where(grade == wanted, 1.0, 0.0), F32).astype(BF16)
            masked[rows, first : first + width] = raw[b, 0:16, 0:width] * keep

    for n in range(4):
        lanes = pl.ds(n * 256, 256)
        plane = jnp.dot(masked[...], maps[:, lanes], preferred_element_type=F32)
        high = plane.astype(BF16)
        low = (plane - high.astype(F32)).astype(BF16)
        for slot in range(16):
            b = brick_of(slot)
            keep = jnp.full((16, 256), jnp.where(levels[0, b] == 2, 1.0, 0.0), F32).astype(BF16)
            here = slice(slot * 16, slot * 16 + 16)
            cells[pl.ds(slot * 32, 16), lanes] = raw[b, 0:16, lanes] * keep + high[here]
            cells[pl.ds(slot * 32 + 16, 16), lanes] = raw[b, 16:32, lanes] * keep + low[here]

    for half in range(2):
        for n in range(4):
            lanes = pl.ds(n * 256, 256)
            dens[half, :, lanes] = jnp.dot(
                zmaps[half], cells[pl.ds(half * 256, 256), lanes], preferred_element_type=F32
            )

    sub = lax.broadcasted_iota(I32, (8, 128), 0)
    lane = lax.broadcasted_iota(I32, (8, 128), 1)
    for copy in fetch_lives:
        copy.wait()
    slopes = [slope[k] * 0.5 for k in range(3)]

    def pixels(half, to):
        return pltpu.make_async_remote_copy(
            src_ref=sends.at[half, to], dst_ref=boxes.at[half, me],
            send_sem=send_sem.at[half], recv_sem=box_sem.at[half],
            device_id={"depth": to}, device_id_type=MESH,
        )

    def send(half, peer, carry):
        pixels(half, swapped(peer)).start()
        return carry

    def along_x(x):
        return pltpu.make_async_remote_copy(
            src_ref=row_send, dst_ref=x_rows.at[my_x], send_sem=row_sem.at[0], recv_sem=row_box.at[0],
            device_id=at_x(x), device_id_type=MESH,
        )

    def along_y(place):
        return pltpu.make_async_remote_copy(
            src_ref=block_send, dst_ref=y_rows.at[my_y], send_sem=row_sem.at[1], recv_sem=row_box.at[1],
            device_id=at_y(place), device_id_type=MESH,
        )

    def start(copy):
        def one(peer, carry):
            copy(peer).start()
            return carry

        return one

    def take(buffer, count, semaphore):
        if count:
            some = buffer.at[pl.ds(0, count)]
            pltpu.make_async_copy(some, some, semaphore).wait()

    packed = jnp.zeros((8, 128), I32)
    for s in range(8):
        packed = jnp.where(sub == s, levels[0, s] + 256 * levels[0, s + 8], packed)
    row_send[...] = packed
    x_rows[my_x] = packed

    source = (lane % 8) * 16 + (lane // 8 % 8) * 2 + lane // 64

    for half in range(2):
        gain = jnp.zeros((8, 128), F32)
        for s in range(8):
            gain = jnp.where(sub == s, -gains[0, brick_of(8 * half + s)], gain)

        def shade(j, carry, half=half, gain=gain):
            lanes = pl.ds(pl.multiple_of(j * 128, 128), 128)
            live = jnp.concatenate(
                [lives[j, pl.ds(8 * half + odd, 4, stride=2), :] for odd in range(2)], axis=0
            )
            tau = jnp.zeros((8, 128), F32)
            through = jnp.ones((8, 128), F32)
            sums = [jnp.zeros((8, 128), F32)] * 3
            for z in range(32):
                x = dens[half, z * 8 : z * 8 + 8, lanes]
                soft = jnp.log(1.0 + jnp.exp(x))
                tau = tau + jnp.where(live > z, soft * gain, 0.0)
                after = jnp.exp(tau)
                glow = through - after
                through = after
                for k in range(3):
                    sums[k] = sums[k] + glow * jnp.tanh(x * slopes[k])
            shaded[0, j], shaded[1, j] = encode(tau, 1.0 - through, sums)
            return carry

        lax.fori_loop(0, 8, shade, 0)

        kinds = []
        for kind in range(2):
            parts = []
            for j in range(8):
                first, second = shaded[0, j], shaded[1, j]
                if kind == 0:
                    words = jnp.where(sub < 4, first, pltpu.roll(second, 4, 0))
                else:
                    words = jnp.where(sub < 4, pltpu.roll(first, 4, 0), second)
                parts.append(jnp.take_along_axis(words, source, axis=1, mode="promise_in_bounds"))
            for bit in range(3):
                step = 1 << bit
                upper = (lane // (8 * step)) % 2 == 1
                for j in range(8):
                    if j & step:
                        continue
                    a, b = parts[j], parts[j + step]
                    parts[j] = jnp.where(upper, pltpu.roll(b, 8 * step, 1), a)
                    parts[j + step] = jnp.where(upper, b, pltpu.roll(a, 128 - 8 * step, 1))
            kinds.append(parts)
        for g in range(8):
            even, odd = kinds[0][g], kinds[1][g]
            sends[half, 2 * g] = jnp.where(lane < 64, even, pltpu.roll(odd, 64, 1))
            sends[half, 2 * g + 1] = jnp.where(lane < 64, pltpu.roll(even, 64, 1), odd)

        if half == 0:
            wait_for(barrier, order + my_x + my_order)
            lax.fori_loop(0, my_x, signal(x_ready, at_x), 0)
            lax.fori_loop(0, my_x, start(along_x), 0)
            lax.fori_loop(0, my_order, signal(y_ready, at_y), 0)
        lax.fori_loop(0, order, functools.partial(send, half), 0)
        boxes[half, me] = sends[half, me]
    lax.fori_loop(0, order, signal(depth_ready, lambda peer: {"depth": swapped(peer)}), 0)

    def serve_later():
        wait_for(depth_ready, depth_count - 1 - order)
        for half in range(2):
            lax.fori_loop(order + 1, depth_count, functools.partial(send, half), 0)

    wait_for(x_ready, x_count - 1 - my_x)
    lax.fori_loop(my_x + 1, x_count, start(along_x), 0)
    pl.when(me >= depth_count // 2)(serve_later)
    take(x_rows, x_count - 1, row_box.at[0])
    table = jnp.zeros((8, 128), I32)
    for x in range(x_count):
        table = jnp.where(lane // y_count == x, x_rows[x], table)
    block_send[...] = table
    y_rows[my_y] = table
    wait_for(y_ready, y_count - 1 - my_order)
    lax.fori_loop(0, my_order, start(along_y), 0)
    lax.fori_loop(my_order + 1, y_count, start(along_y), 0)
    take(y_rows, y_count - 1, row_box.at[1])
    for y in range(y_count):
        table = jnp.where(lane % y_count == y, y_rows[y], table)
    table = table[:, 0:tile_count]
    total = jnp.zeros((8, tile_count), F32)
    for part, grade in enumerate((table & 255, table >> 8)):
        worth = jnp.where(grade == 2, 1.0, jnp.where(grade == 1, 0.25, 0.0625))
        total = total + jnp.where(owners[8 * part : 8 * part + 8] == tile, worth, 0.0)
    share[...] = jnp.sum(total, keepdims=True) * (1.0 / 16.0)

    pl.when(me < depth_count // 2)(serve_later)

    take(x_rows, x_count - 1, row_sem.at[0])
    take(y_rows, y_count - 1, row_sem.at[1])
    for half in range(2):
        take(sends.at[half], depth_count - 1, send_sem.at[half])
    for half in range(2):
        take(boxes.at[half], depth_count - 1, box_sem.at[half])


def composite_kernel(depth_count, boxes, share_in, out, share):
    low = lax.broadcasted_iota(I32, (8, 128), 0) < 4
    passed, even, odd = [], [], []
    for half in range(2):
        ahead = jnp.ones((8, 128), F32)
        first = jnp.zeros((8, 128), F32)
        second = jnp.zeros((8, 128), F32)
        for d in range(depth_count):
            word = boxes[half, d]
            bottom = (word & 65535).astype(F32)
            top = lax.shift_right_logical(word, 16).astype(F32)
            code = jnp.where(low, pltpu.roll(top, 4, 0), top)
            through = jnp.exp(-jnp.exp2(code * (1.0 / CODE_SCALE) + CODE_FLOOR))
            weight = ahead * (1.0 - through)
            first = first + weight * bottom
            second = second + weight * top
            ahead = ahead * through
        passed.append(ahead)
        even.append(first * (1.0 / 65535.0))
        odd.append(second * (1.0 / 65535.0))
    out[0] = jnp.where(low, even[0], pltpu.roll(even[1], 4, 0))
    out[1] = jnp.where(low, odd[0], pltpu.roll(odd[1], 4, 0))
    out[2] = jnp.where(low, pltpu.roll(even[0], 4, 0), even[1])
    out[3] = 1.0 - jnp.where(low, passed[0], passed[1])
    share[...] = share_in[...]


def local(bricks, levels, counts, gains, ownership, tf_slope):
    depth_count = lax.axis_size("depth")
    tile_count = lax.axis_size("tile")
    y_count = min(8, tile_count)
    x_count = tile_count // y_count
    vmem = pl.BlockSpec(memory_space=pltpu.VMEM)
    anywhere = pl.BlockSpec(memory_space=pltpu.HBM)
    dma = pltpu.SemaphoreType.DMA
    boxes, share = pl.pallas_call(
        functools.partial(kernel, depth_count, x_count, y_count),
        out_shape=(
            pltpu.VMEM((2, 16, 8, 128), I32),
            pltpu.VMEM((1, 1), F32),
        ),
        in_specs=[anywhere] * 6,
        out_specs=(vmem, vmem),
        scratch_shapes=[
            pltpu.SMEM((1, 16), I32),
            pltpu.SMEM((1, 16), F32),
            pltpu.SMEM((3,), F32),
            pltpu.VMEM((16, tile_count), I32),
            pltpu.VMEM((16, 32, 1024), BF16),
            pltpu.VMEM((8, 16, 128), I32),
            pltpu.VMEM((256, 768), BF16),
            pltpu.VMEM((768, 1024), BF16),
            pltpu.VMEM((512, 1024), BF16),
            pltpu.VMEM((2, 256, 256), BF16),
            pltpu.VMEM((2, 256, 1024), F32),
            pltpu.VMEM((2, 8, 8, 128), I32),
            pltpu.VMEM((2, 16, 8, 128), I32),
            pltpu.VMEM((8, 128), I32),
            pltpu.VMEM((8, 128), I32),
            pltpu.VMEM((x_count, 8, 128), I32),
            pltpu.VMEM((y_count, 8, 128), I32),
            dma((4,)),
            dma((4,)),
            dma((8,)),
            dma((2,)),
            dma((2,)),
            dma((2,)),
            dma((2,)),
            pltpu.SemaphoreType.REGULAR,
            pltpu.SemaphoreType.REGULAR,
            pltpu.SemaphoreType.REGULAR,
        ],
        compiler_params=pltpu.CompilerParams(
            collective_id=0, has_side_effects=True, vmem_limit_bytes=56000 * 1024
        ),
        name="render",
    )(bricks, levels, counts, gains, jnp.swapaxes(ownership, 1, 2), tf_slope)
    composite, share = pl.pallas_call(
        functools.partial(composite_kernel, depth_count),
        out_shape=(
            jax.ShapeDtypeStruct((4, 8, 128), F32),
            jax.ShapeDtypeStruct((1, 1), F32),
        ),
        in_specs=[vmem, vmem],
        out_specs=(vmem, vmem),
        compiler_params=pltpu.CompilerParams(vmem_limit_bytes=4 * 1024 * 1024),
        name="composite",
    )(boxes, share)
    return composite.reshape(4, 1, 1024), share


def solution(mesh):
    placed = (
        P("depth", "tile", None, None),
        P("depth", "tile"),
        P("depth", "tile", None),
        P("depth", "tile"),
        P("depth", None, None),
        P(),
    )
    return jax.shard_map(
        local,
        mesh=mesh,
        in_specs=placed,
        out_specs=(P(None, "depth", "tile"), P("depth", "tile")),
        check_vma=False,
    )
```

```python
import functools

import jax
import jax.numpy as jnp
from jax import lax
from jax.experimental import pallas as pl
from jax.experimental.pallas import tpu as pltpu
from jax.sharding import PartitionSpec as P

F32 = jnp.float32
BF16 = jnp.bfloat16
I32 = jnp.int32
MESH = pl.DeviceIdType.MESH
CODE_FLOOR = -20.75
CODE_SCALE = 65535.0 / 23.75


def tent(at, cell):
    return jnp.maximum(0.0, 1.0 - jnp.abs(at - cell))


def coarse_at(fine, side):
    return jnp.clip((fine + 0.5) * (side / 32.0) - 0.5, 0.0, side - 1.0)


def fill_plane_maps(maps):
    lane = lax.broadcasted_iota(I32, (8, 1024), 1)
    y_of = (lane // 32).astype(F32)
    x_of = lax.broadcasted_iota(I32, (32, 128), 1) % 32
    e_of = lax.broadcasted_iota(I32, (32, 128), 0).astype(F32)
    for first, side in ((0, 8), (256, 16)):
        along_x = tent(coarse_at(x_of.astype(F32), side), e_of)
        along_x = jnp.concatenate([along_x] * 8, axis=1)
        y_at = coarse_at(y_of, side)

        def one(c, carry, first=first, along_x=along_x, y_at=y_at):
            along_y = tent(y_at, c.astype(F32))
            both = along_x * jnp.concatenate([along_y] * 4, axis=0)
            maps[pl.ds(pl.multiple_of(first + c * 32, 32), 32), :] = both.astype(BF16)
            return carry

        lax.fori_loop(0, side, one, 0)


def brick_of(slot):
    half, place = slot // 8, slot % 8
    return 8 * half + 2 * (place % 4) + place // 4


def depth_map(levels, half):
    lane = lax.broadcasted_iota(I32, (1, 256), 1)
    slot = lane // 32
    grade = jnp.zeros((1, 256), I32)
    for s in range(8):
        grade = jnp.where(slot == s, levels[0, brick_of(8 * half + s)], grade)
    side = jnp.where(grade == 2, 32.0, jnp.where(grade == 1, 16.0, 8.0))
    cell = lane % 32
    cell = jnp.where(grade == 2, cell, cell % 16).astype(F32)
    row = lax.broadcasted_iota(I32, (256, 256), 0)
    z_of = (row // 8).astype(F32)
    at = jnp.minimum(jnp.maximum((z_of + 0.5) * (side / 32.0) - 0.5, 0.0), side - 1.0)
    same = (row % 8) == (lax.broadcasted_iota(I32, (256, 256), 1) // 32)
    return jnp.where(same, tent(at, cell), 0.0).astype(BF16)


def encode(tau, solid, sums):
    scale = 32767.5 / jnp.maximum(solid, 1e-12)
    codes = [
        jnp.clip(sums[k] * scale + 32768.0, 0.0, 65535.0).astype(I32) for k in range(3)
    ]
    depth = jnp.log2(jnp.maximum(-tau, 1e-12))
    codes.append(jnp.clip((depth - CODE_FLOOR) * CODE_SCALE + 0.5, 0.0, 65535.0).astype(I32))
    return codes[0] | (codes[1] << 16), codes[2] | (codes[3] << 16)


def swapped(place):
    return place + 1 - 2 * (place % 2)


def wait_for(semaphore, count):
    @pl.when(count > 0)
    def _():
        pl.semaphore_wait(semaphore, count)


def y_order(y, count):
    back = count - y
    return jnp.where(y <= back, jnp.maximum(2 * y - 1, 0), 2 * back)


def y_at(order, count):
    return jnp.where(order % 2 == 1, (order + 1) // 2, (count - order // 2) % count)


def kernel(
    depth_count, x_count, y_count,
    bricks, levels_in, counts, gains_in, owners_in, slope_in,
    boxes, share,
    levels, gains, slope, owners,
    raw, lives, masked, maps, cells, zmaps, dens, shaded, sends,
    row_send, block_send, x_rows, y_rows,
    small_sem, brick_sem, live_sem, send_sem, box_sem,
    row_sem, row_box, depth_ready, x_ready, y_ready,
):
    me = lax.axis_index("depth")
    tile = lax.axis_index("tile")
    tile_count = x_count * y_count
    my_x, my_y = tile // y_count, tile % y_count

    fetch_small = [
        pltpu.make_async_copy(there, here, small_sem.at[i])
        for i, (there, here) in enumerate(
            ((levels_in, levels), (gains_in, gains), (slope_in, slope), (owners_in.at[0], owners))
        )
    ]
    fetch_bricks = [
        pltpu.make_async_copy(bricks.at[0, pl.ds(i * 4, 4)], raw.at[pl.ds(i * 4, 4)], brick_sem.at[i])
        for i in range(4)
    ]
    fetch_lives = [
        pltpu.make_async_copy(counts.at[0, :, pl.ds(j * 128, 128)], lives.at[j], live_sem.at[j])
        for j in range(8)
    ]
    for copy in fetch_bricks + fetch_small + fetch_lives:
        copy.start()

    barrier = pltpu.get_barrier_semaphore()
    order = swapped(me)

    def greet(peer, carry):
        pl.semaphore_signal(barrier, inc=1, device_id={"depth": swapped(peer)}, device_id_type=MESH)
        return carry

    lax.fori_loop(order + 1, depth_count, greet, 0)
    my_order = y_order(my_y, y_count)

    def at_x(x):
        return {"tile": x * y_count + my_y}

    def at_y(place):
        return {"tile": my_x * y_count + y_at(place, y_count)}

    def signal(semaphore, device):
        def one(peer, carry):
            pl.semaphore_signal(semaphore, inc=1, device_id=device(peer), device_id_type=MESH)
            return carry

        return one

    lax.fori_loop(my_x + 1, x_count, signal(barrier, at_x), 0)
    lax.fori_loop(my_order + 1, y_count, signal(barrier, at_y), 0)

    fill_plane_maps(maps)
    for copy in fetch_small:
        copy.wait()
    for half in range(2):
        zmaps[half] = depth_map(levels, half)

    for copy in fetch_bricks:
        copy.wait()
    for slot in range(16):
        b = brick_of(slot)
        grade = levels[0, b]
        rows = pl.ds(slot * 16, 16)
        for first, width, wanted in ((0, 256, 0), (256, 512, 1)):
            keep = jnp.full((16, width), jnp.where(grade == wanted, 1.0, 0.0), F32).astype(BF16)
            masked[rows, first : first + width] = raw[b, 0:16, 0:width] * keep

    for n in range(4):
        lanes = pl.ds(n * 256, 256)
        plane = jnp.dot(masked[...], maps[:, lanes], preferred_element_type=F32)
        high = plane.astype(BF16)
        low = (plane - high.astype(F32)).astype(BF16)
        for slot in range(16):
            b = brick_of(slot)
            keep = jnp.full((16, 256), jnp.where(levels[0, b] == 2, 1.0, 0.0), F32).astype(BF16)
            here = slice(slot * 16, slot * 16 + 16)
            cells[pl.ds(slot * 32, 16), lanes] = raw[b, 0:16, lanes] * keep + high[here]
            cells[pl.ds(slot * 32 + 16, 16), lanes] = raw[b, 16:32, lanes] * keep + low[here]

    for half in range(2):
        for n in range(4):
            lanes = pl.ds(n * 256, 256)
            dens[half, :, lanes] = jnp.dot(
                zmaps[half], cells[pl.ds(half * 256, 256), lanes], preferred_element_type=F32
            )

    sub = lax.broadcasted_iota(I32, (8, 128), 0)
    lane = lax.broadcasted_iota(I32, (8, 128), 1)
    for copy in fetch_lives:
        copy.wait()
    slopes = [slope[k] * 0.5 for k in range(3)]

    def pixels(half, to):
        return pltpu.make_async_remote_copy(
            src_ref=sends.at[half, to], dst_ref=boxes.at[half, me],
            send_sem=send_sem.at[half], recv_sem=box_sem.at[half],
            device_id={"depth": to}, device_id_type=MESH,
        )

    def send(half, peer, carry):
        pixels(half, swapped(peer)).start()
        return carry

    def along_x(x):
        return pltpu.make_async_remote_copy(
            src_ref=row_send, dst_ref=x_rows.at[my_x], send_sem=row_sem.at[0], recv_sem=row_box.at[0],
            device_id=at_x(x), device_id_type=MESH,
        )

    def along_y(place):
        return pltpu.make_async_remote_copy(
            src_ref=block_send, dst_ref=y_rows.at[my_y], send_sem=row_sem.at[1], recv_sem=row_box.at[1],
            device_id=at_y(place), device_id_type=MESH,
        )

    def start(copy):
        def one(peer, carry):
            copy(peer).start()
            return carry

        return one

    def take(buffer, count, semaphore):
        if count:
            some = buffer.at[pl.ds(0, count)]
            pltpu.make_async_copy(some, some, semaphore).wait()

    packed = jnp.zeros((8, 128), I32)
    for s in range(8):
        packed = jnp.where(sub == s, levels[0, s] + 256 * levels[0, s + 8], packed)
    row_send[...] = packed
    x_rows[my_x] = packed

    source = (lane % 8) * 16 + (lane // 8 % 8) * 2 + lane // 64

    for half in range(2):
        gain = jnp.zeros((8, 128), F32)
        for s in range(8):
            gain = jnp.where(sub == s, -gains[0, brick_of(8 * half + s)], gain)

        def shade(j, carry, half=half, gain=gain):
            lanes = pl.ds(pl.multiple_of(j * 128, 128), 128)
            live = jnp.concatenate(
                [lives[j, pl.ds(8 * half + odd, 4, stride=2), :] for odd in range(2)], axis=0
            )
            tau = jnp.zeros((8, 128), F32)
            through = jnp.ones((8, 128), F32)
            sums = [jnp.zeros((8, 128), F32)] * 3
            for z in range(32):
                x = dens[half, z * 8 : z * 8 + 8, lanes]
                soft = jnp.log(1.0 + jnp.exp(x))
                tau = tau + jnp.where(live > z, soft * gain, 0.0)
                after = jnp.exp(tau)
                glow = through - after
                through = after
                for k in range(3):
                    sums[k] = sums[k] + glow * jnp.tanh(x * slopes[k])
            shaded[0, j], shaded[1, j] = encode(tau, 1.0 - through, sums)
            return carry

        lax.fori_loop(0, 8, shade, 0)

        kinds = []
        for kind in range(2):
            parts = []
            for j in range(8):
                first, second = shaded[0, j], shaded[1, j]
                if kind == 0:
                    words = jnp.where(sub < 4, first, pltpu.roll(second, 4, 0))
                else:
                    words = jnp.where(sub < 4, pltpu.roll(first, 4, 0), second)
                parts.append(jnp.take_along_axis(words, source, axis=1, mode="promise_in_bounds"))
            for bit in range(3):
                step = 1 << bit
                upper = (lane // (8 * step)) % 2 == 1
                for j in range(8):
                    if j & step:
                        continue
                    a, b = parts[j], parts[j + step]
                    parts[j] = jnp.where(upper, pltpu.roll(b, 8 * step, 1), a)
                    parts[j + step] = jnp.where(upper, b, pltpu.roll(a, 128 - 8 * step, 1))
            kinds.append(parts)
        for g in range(8):
            even, odd = kinds[0][g], kinds[1][g]
            sends[half, 2 * g] = jnp.where(lane < 64, even, pltpu.roll(odd, 64, 1))
            sends[half, 2 * g + 1] = jnp.where(lane < 64, pltpu.roll(even, 64, 1), odd)

        if half == 0:
            wait_for(barrier, order + my_x + my_order)
            lax.fori_loop(0, my_x, signal(x_ready, at_x), 0)
            lax.fori_loop(0, my_x, start(along_x), 0)
            lax.fori_loop(0, my_order, signal(y_ready, at_y), 0)
        lax.fori_loop(0, order, functools.partial(send, half), 0)
        boxes[half, me] = sends[half, me]
        if half == 0:
            lax.fori_loop(0, order, signal(depth_ready, lambda peer: {"depth": swapped(peer)}), 0)

    def serve_later():
        wait_for(depth_ready, depth_count - 1 - order)
        for half in range(2):
            lax.fori_loop(order + 1, depth_count, functools.partial(send, half), 0)

    wait_for(x_ready, x_count - 1 - my_x)
    lax.fori_loop(my_x + 1, x_count, start(along_x), 0)
    pl.when(me >= depth_count // 2)(serve_later)
    take(x_rows, x_count - 1, row_box.at[0])
    table = jnp.zeros((8, 128), I32)
    for x in range(x_count):
        table = jnp.where(lane // y_count == x, x_rows[x], table)
    block_send[...] = table
    y_rows[my_y] = table
    wait_for(y_ready, y_count - 1 - my_order)
    lax.fori_loop(0, my_order, start(along_y), 0)
    lax.fori_loop(my_order + 1, y_count, start(along_y), 0)
    pl.when(me < depth_count // 2)(serve_later)
    take(y_rows, y_count - 1, row_box.at[1])
    for y in range(y_count):
        table = jnp.where(lane % y_count == y, y_rows[y], table)
    table = table[:, 0:tile_count]
    total = jnp.zeros((8, tile_count), F32)
    for part, grade in enumerate((table & 255, table >> 8)):
        worth = jnp.where(grade == 2, 1.0, jnp.where(grade == 1, 0.25, 0.0625))
        total = total + jnp.where(owners[8 * part : 8 * part + 8] == tile, worth, 0.0)
    share[...] = jnp.sum(total, keepdims=True) * (1.0 / 16.0)

    take(x_rows, x_count - 1, row_sem.at[0])
    take(y_rows, y_count - 1, row_sem.at[1])
    for half in range(2):
        take(sends.at[half], depth_count - 1, send_sem.at[half])
    for half in range(2):
        take(boxes.at[half], depth_count - 1, box_sem.at[half])


def composite_kernel(depth_count, boxes, share_in, out, share):
    low = lax.broadcasted_iota(I32, (8, 128), 0) < 4
    passed, even, odd = [], [], []
    for half in range(2):
        ahead = jnp.ones((8, 128), F32)
        first = jnp.zeros((8, 128), F32)
        second = jnp.zeros((8, 128), F32)
        for d in range(depth_count):
            word = boxes[half, d]
            bottom = (word & 65535).astype(F32)
            top = lax.shift_right_logical(word, 16).astype(F32)
            code = jnp.where(low, pltpu.roll(top, 4, 0), top)
            through = jnp.exp(-jnp.exp2(code * (1.0 / CODE_SCALE) + CODE_FLOOR))
            weight = ahead * (1.0 - through)
            first = first + weight * bottom
            second = second + weight * top
            ahead = ahead * through
        passed.append(ahead)
        even.append(first * (1.0 / 65535.0))
        odd.append(second * (1.0 / 65535.0))
    out[0] = jnp.where(low, even[0], pltpu.roll(even[1], 4, 0))
    out[1] = jnp.where(low, odd[0], pltpu.roll(odd[1], 4, 0))
    out[2] = jnp.where(low, pltpu.roll(even[0], 4, 0), even[1])
    out[3] = 1.0 - jnp.where(low, passed[0], passed[1])
    share[...] = share_in[...]


def local(bricks, levels, counts, gains, ownership, tf_slope):
    depth_count = lax.axis_size("depth")
    tile_count = lax.axis_size("tile")
    y_count = min(8, tile_count)
    x_count = tile_count // y_count
    vmem = pl.BlockSpec(memory_space=pltpu.VMEM)
    anywhere = pl.BlockSpec(memory_space=pltpu.HBM)
    dma = pltpu.SemaphoreType.DMA
    boxes, share = pl.pallas_call(
        functools.partial(kernel, depth_count, x_count, y_count),
        out_shape=(
            pltpu.VMEM((2, 16, 8, 128), I32),
            pltpu.VMEM((1, 1), F32),
        ),
        in_specs=[anywhere] * 6,
        out_specs=(vmem, vmem),
        scratch_shapes=[
            pltpu.SMEM((1, 16), I32),
            pltpu.SMEM((1, 16), F32),
            pltpu.SMEM((3,), F32),
            pltpu.VMEM((16, tile_count), I32),
            pltpu.VMEM((16, 32, 1024), BF16),
            pltpu.VMEM((8, 16, 128), I32),
            pltpu.VMEM((256, 768), BF16),
            pltpu.VMEM((768, 1024), BF16),
            pltpu.VMEM((512, 1024), BF16),
            pltpu.VMEM((2, 256, 256), BF16),
            pltpu.VMEM((2, 256, 1024), F32),
            pltpu.VMEM((2, 8, 8, 128), I32),
            pltpu.VMEM((2, 16, 8, 128), I32),
            pltpu.VMEM((8, 128), I32),
            pltpu.VMEM((8, 128), I32),
            pltpu.VMEM((x_count, 8, 128), I32),
            pltpu.VMEM((y_count, 8, 128), I32),
            dma((4,)),
            dma((4,)),
            dma((8,)),
            dma((2,)),
            dma((2,)),
            dma((2,)),
            dma((2,)),
            pltpu.SemaphoreType.REGULAR,
            pltpu.SemaphoreType.REGULAR,
            pltpu.SemaphoreType.REGULAR,
        ],
        compiler_params=pltpu.CompilerParams(
            collective_id=0, has_side_effects=True, vmem_limit_bytes=56000 * 1024
        ),
        name="render",
    )(bricks, levels, counts, gains, jnp.swapaxes(ownership, 1, 2), tf_slope)
    composite, share = pl.pallas_call(
        functools.partial(composite_kernel, depth_count),
        out_shape=(
            jax.ShapeDtypeStruct((4, 8, 128), F32),
            jax.ShapeDtypeStruct((1, 1), F32),
        ),
        in_specs=[vmem, vmem],
        out_specs=(vmem, vmem),
        compiler_params=pltpu.CompilerParams(vmem_limit_bytes=4 * 1024 * 1024),
        name="composite",
    )(boxes, share)
    return composite.reshape(4, 1, 1024), share


def solution(mesh):
    placed = (
        P("depth", "tile", None, None),
        P("depth", "tile"),
        P("depth", "tile", None),
        P("depth", "tile"),
        P("depth", None, None),
        P(),
    )
    return jax.shard_map(
        local,
        mesh=mesh,
        in_specs=placed,
        out_specs=(P(None, "depth", "tile"), P("depth", "tile")),
        check_vma=False,
    )
```

```python
import functools

import jax
import jax.numpy as jnp
from jax import lax
from jax.experimental import pallas as pl
from jax.experimental.pallas import tpu as pltpu
from jax.sharding import PartitionSpec as P

F32 = jnp.float32
BF16 = jnp.bfloat16
I32 = jnp.int32
MESH = pl.DeviceIdType.MESH
CODE_FLOOR = -20.75
CODE_SCALE = 65535.0 / 23.75


def tent(at, cell):
    return jnp.maximum(0.0, 1.0 - jnp.abs(at - cell))


def coarse_at(fine, side):
    return jnp.clip((fine + 0.5) * (side / 32.0) - 0.5, 0.0, side - 1.0)


def fill_plane_maps(maps):
    lane = lax.broadcasted_iota(I32, (8, 1024), 1)
    y_of = (lane // 32).astype(F32)
    x_of = lax.broadcasted_iota(I32, (32, 128), 1) % 32
    e_of = lax.broadcasted_iota(I32, (32, 128), 0).astype(F32)
    for first, side in ((0, 8), (256, 16)):
        along_x = tent(coarse_at(x_of.astype(F32), side), e_of)
        along_x = jnp.concatenate([along_x] * 8, axis=1)
        y_at = coarse_at(y_of, side)

        def one(c, carry, first=first, along_x=along_x, y_at=y_at):
            along_y = tent(y_at, c.astype(F32))
            both = along_x * jnp.concatenate([along_y] * 4, axis=0)
            maps[pl.ds(pl.multiple_of(first + c * 32, 32), 32), :] = both.astype(BF16)
            return carry

        lax.fori_loop(0, side, one, 0)


def brick_of(slot):
    half, place = slot // 8, slot % 8
    return 8 * half + 2 * (place % 4) + place // 4


def depth_map(levels, half):
    lane = lax.broadcasted_iota(I32, (1, 256), 1)
    slot = lane // 32
    grade = jnp.zeros((1, 256), I32)
    for s in range(8):
        grade = jnp.where(slot == s, levels[0, brick_of(8 * half + s)], grade)
    side = jnp.where(grade == 2, 32.0, jnp.where(grade == 1, 16.0, 8.0))
    cell = lane % 32
    cell = jnp.where(grade == 2, cell, cell % 16).astype(F32)
    row = lax.broadcasted_iota(I32, (256, 256), 0)
    z_of = (row // 8).astype(F32)
    at = jnp.minimum(jnp.maximum((z_of + 0.5) * (side / 32.0) - 0.5, 0.0), side - 1.0)
    same = (row % 8) == (lax.broadcasted_iota(I32, (256, 256), 1) // 32)
    return jnp.where(same, tent(at, cell), 0.0).astype(BF16)


def encode(tau, solid, sums):
    scale = 32767.5 / jnp.maximum(solid, 1e-12)
    codes = [
        jnp.clip(sums[k] * scale + 32768.0, 0.0, 65535.0).astype(I32) for k in range(3)
    ]
    depth = jnp.log2(jnp.maximum(-tau, 1e-12))
    codes.append(jnp.clip((depth - CODE_FLOOR) * CODE_SCALE + 0.5, 0.0, 65535.0).astype(I32))
    return codes[0] | (codes[1] << 16), codes[2] | (codes[3] << 16)


def swapped(place):
    return place + 1 - 2 * (place % 2)


def wait_for(semaphore, count):
    @pl.when(count > 0)
    def _():
        pl.semaphore_wait(semaphore, count)


def y_order(y, count):
    back = count - y
    return jnp.where(y <= back, jnp.maximum(2 * y - 1, 0), 2 * back)


def y_at(order, count):
    return jnp.where(order % 2 == 1, (order + 1) // 2, (count - order // 2) % count)


def kernel(
    depth_count, x_count, y_count,
    bricks, levels_in, counts, gains_in, owners_in, slope_in,
    out, share,
    levels, gains, slope, owners,
    raw, lives, masked, maps, cells, zmaps, dens, shaded, sends,
    row_send, block_send, x_rows, y_rows, boxes,
    small_sem, brick_sem, live_sem, send_sem, box_sem,
    row_sem, row_box, depth_ready, x_ready, y_ready,
):
    me = lax.axis_index("depth")
    tile = lax.axis_index("tile")
    tile_count = x_count * y_count
    my_x, my_y = tile // y_count, tile % y_count

    fetch_small = [
        pltpu.make_async_copy(there, here, small_sem.at[i])
        for i, (there, here) in enumerate(
            ((levels_in, levels), (gains_in, gains), (slope_in, slope), (owners_in.at[0], owners))
        )
    ]
    fetch_bricks = [
        pltpu.make_async_copy(bricks.at[0, pl.ds(i * 4, 4)], raw.at[pl.ds(i * 4, 4)], brick_sem.at[i])
        for i in range(4)
    ]
    fetch_lives = [
        pltpu.make_async_copy(counts.at[0, :, pl.ds(j * 128, 128)], lives.at[j], live_sem.at[j])
        for j in range(8)
    ]
    for copy in fetch_bricks + fetch_small + fetch_lives:
        copy.start()

    barrier = pltpu.get_barrier_semaphore()
    order = swapped(me)

    def greet(peer, carry):
        pl.semaphore_signal(barrier, inc=1, device_id={"depth": swapped(peer)}, device_id_type=MESH)
        return carry

    lax.fori_loop(order + 1, depth_count, greet, 0)
    my_order = y_order(my_y, y_count)

    def at_x(x):
        return {"tile": x * y_count + my_y}

    def at_y(place):
        return {"tile": my_x * y_count + y_at(place, y_count)}

    def signal(semaphore, device):
        def one(peer, carry):
            pl.semaphore_signal(semaphore, inc=1, device_id=device(peer), device_id_type=MESH)
            return carry

        return one

    lax.fori_loop(my_x + 1, x_count, signal(barrier, at_x), 0)
    lax.fori_loop(my_order + 1, y_count, signal(barrier, at_y), 0)

    fill_plane_maps(maps)
    for copy in fetch_small:
        copy.wait()
    for half in range(2):
        zmaps[half] = depth_map(levels, half)

    for copy in fetch_bricks:
        copy.wait()
    for slot in range(16):
        b = brick_of(slot)
        grade = levels[0, b]
        rows = pl.ds(slot * 16, 16)
        for first, width, wanted in ((0, 256, 0), (256, 512, 1)):
            keep = jnp.full((16, width), jnp.where(grade == wanted, 1.0, 0.0), F32).astype(BF16)
            masked[rows, first : first + width] = raw[b, 0:16, 0:width] * keep

    for n in range(4):
        lanes = pl.ds(n * 256, 256)
        plane = jnp.dot(masked[...], maps[:, lanes], preferred_element_type=F32)
        high = plane.astype(BF16)
        low = (plane - high.astype(F32)).astype(BF16)
        for slot in range(16):
            b = brick_of(slot)
            keep = jnp.full((16, 256), jnp.where(levels[0, b] == 2, 1.0, 0.0), F32).astype(BF16)
            here = slice(slot * 16, slot * 16 + 16)
            cells[pl.ds(slot * 32, 16), lanes] = raw[b, 0:16, lanes] * keep + high[here]
            cells[pl.ds(slot * 32 + 16, 16), lanes] = raw[b, 16:32, lanes] * keep + low[here]

    for half in range(2):
        for n in range(4):
            lanes = pl.ds(n * 256, 256)
            dens[half, :, lanes] = jnp.dot(
                zmaps[half], cells[pl.ds(half * 256, 256), lanes], preferred_element_type=F32
            )

    sub = lax.broadcasted_iota(I32, (8, 128), 0)
    lane = lax.broadcasted_iota(I32, (8, 128), 1)
    for copy in fetch_lives:
        copy.wait()
    slopes = [slope[k] * 0.5 for k in range(3)]

    def pixels(half, to):
        return pltpu.make_async_remote_copy(
            src_ref=sends.at[half, to], dst_ref=boxes.at[half, me],
            send_sem=send_sem.at[half], recv_sem=box_sem.at[half],
            device_id={"depth": to}, device_id_type=MESH,
        )

    def send(half, peer, carry):
        pixels(half, swapped(peer)).start()
        return carry

    def along_x(x):
        return pltpu.make_async_remote_copy(
            src_ref=row_send, dst_ref=x_rows.at[my_x], send_sem=row_sem.at[0], recv_sem=row_box.at[0],
            device_id=at_x(x), device_id_type=MESH,
        )

    def along_y(place):
        return pltpu.make_async_remote_copy(
            src_ref=block_send, dst_ref=y_rows.at[my_y], send_sem=row_sem.at[1], recv_sem=row_box.at[1],
            device_id=at_y(place), device_id_type=MESH,
        )

    def start(copy):
        def one(peer, carry):
            copy(peer).start()
            return carry

        return one

    def take(buffer, count, semaphore):
        if count:
            some = buffer.at[pl.ds(0, count)]
            pltpu.make_async_copy(some, some, semaphore).wait()

    packed = jnp.zeros((8, 128), I32)
    for s in range(8):
        packed = jnp.where(sub == s, levels[0, s] + 256 * levels[0, s + 8], packed)
    row_send[...] = packed
    x_rows[my_x] = packed

    source = (lane % 8) * 16 + (lane // 8 % 8) * 2 + lane // 64

    for half in range(2):
        gain = jnp.zeros((8, 128), F32)
        for s in range(8):
            gain = jnp.where(sub == s, -gains[0, brick_of(8 * half + s)], gain)

        gain = jnp.concatenate([gain, gain], axis=1)

        def shade(n, carry, half=half, gain=gain):
            lanes = pl.ds(pl.multiple_of(n * 256, 256), 256)
            live = jnp.concatenate(
                [
                    jnp.concatenate(
                        [lives[2 * n + j, pl.ds(8 * half + odd, 4, stride=2), :] for odd in range(2)], axis=0
                    )
                    for j in range(2)
                ],
                axis=1,
            )
            tau = jnp.zeros((8, 256), F32)
            through = jnp.ones((8, 256), F32)
            sums = [jnp.zeros((8, 256), F32)] * 3
            for z in range(32):
                x = dens[half, z * 8 : z * 8 + 8, lanes]
                soft = jnp.log(1.0 + jnp.exp(x))
                tau = tau + jnp.where(live > z, soft * gain, 0.0)
                after = jnp.exp(tau)
                glow = through - after
                through = after
                for k in range(3):
                    sums[k] = sums[k] + glow * jnp.tanh(x * slopes[k])
            for k, words in enumerate(encode(tau, 1.0 - through, sums)):
                for j in range(2):
                    shaded[k, 2 * n + j] = words[:, 128 * j : 128 * j + 128]
            return carry

        lax.fori_loop(0, 4, shade, 0)

        kinds = []
        for kind in range(2):
            parts = []
            for j in range(8):
                first, second = shaded[0, j], shaded[1, j]
                if kind == 0:
                    words = jnp.where(sub < 4, first, pltpu.roll(second, 4, 0))
                else:
                    words = jnp.where(sub < 4, pltpu.roll(first, 4, 0), second)
                parts.append(jnp.take_along_axis(words, source, axis=1, mode="promise_in_bounds"))
            for bit in range(3):
                step = 1 << bit
                upper = (lane // (8 * step)) % 2 == 1
                for j in range(8):
                    if j & step:
                        continue
                    a, b = parts[j], parts[j + step]
                    parts[j] = jnp.where(upper, pltpu.roll(b, 8 * step, 1), a)
                    parts[j + step] = jnp.where(upper, b, pltpu.roll(a, 128 - 8 * step, 1))
            kinds.append(parts)
        for g in range(8):
            even, odd = kinds[0][g], kinds[1][g]
            sends[half, 2 * g] = jnp.where(lane < 64, even, pltpu.roll(odd, 64, 1))
            sends[half, 2 * g + 1] = jnp.where(lane < 64, pltpu.roll(even, 64, 1), odd)

        if half == 0:
            wait_for(barrier, order + my_x + my_order)
            lax.fori_loop(0, my_x, signal(x_ready, at_x), 0)
            lax.fori_loop(0, my_x, start(along_x), 0)
            lax.fori_loop(0, my_order, signal(y_ready, at_y), 0)
        lax.fori_loop(0, order, functools.partial(send, half), 0)
        boxes[half, me] = sends[half, me]
        if half == 0:
            lax.fori_loop(0, order, signal(depth_ready, lambda peer: {"depth": swapped(peer)}), 0)

    def serve_later():
        wait_for(depth_ready, depth_count - 1 - order)
        for half in range(2):
            lax.fori_loop(order + 1, depth_count, functools.partial(send, half), 0)

    wait_for(x_ready, x_count - 1 - my_x)
    lax.fori_loop(my_x + 1, x_count, start(along_x), 0)
    pl.when(me >= depth_count // 2)(serve_later)
    take(x_rows, x_count - 1, row_box.at[0])
    table = jnp.zeros((8, 128), I32)
    for x in range(x_count):
        table = jnp.where(lane // y_count == x, x_rows[x], table)
    block_send[...] = table
    y_rows[my_y] = table
    wait_for(y_ready, y_count - 1 - my_order)
    lax.fori_loop(0, my_order, start(along_y), 0)
    lax.fori_loop(my_order + 1, y_count, start(along_y), 0)
    pl.when(me < depth_count // 2)(serve_later)
    take(y_rows, y_count - 1, row_box.at[1])
    for y in range(y_count):
        table = jnp.where(lane % y_count == y, y_rows[y], table)
    table = table[:, 0:tile_count]
    total = jnp.zeros((8, tile_count), F32)
    for part, grade in enumerate((table & 255, table >> 8)):
        worth = jnp.where(grade == 2, 1.0, jnp.where(grade == 1, 0.25, 0.0625))
        total = total + jnp.where(owners[8 * part : 8 * part + 8] == tile, worth, 0.0)
    share[...] = jnp.sum(total, keepdims=True) * (1.0 / 16.0)

    take(x_rows, x_count - 1, row_sem.at[0])
    take(y_rows, y_count - 1, row_sem.at[1])
    for half in range(2):
        take(sends.at[half], depth_count - 1, send_sem.at[half])
    for half in range(2):
        take(boxes.at[half], depth_count - 1, box_sem.at[half])
    low = lax.broadcasted_iota(I32, (8, 128), 0) < 4
    passed, even, odd = [], [], []
    for half in range(2):
        ahead = jnp.ones((8, 128), F32)
        first = jnp.zeros((8, 128), F32)
        second = jnp.zeros((8, 128), F32)
        for d in range(depth_count):
            word = boxes[half, d]
            bottom = (word & 65535).astype(F32)
            top = lax.shift_right_logical(word, 16).astype(F32)
            code = jnp.where(low, pltpu.roll(top, 4, 0), top)
            through = jnp.exp(-jnp.exp2(code * (1.0 / CODE_SCALE) + CODE_FLOOR))
            weight = ahead * (1.0 - through)
            first = first + weight * bottom
            second = second + weight * top
            ahead = ahead * through
        passed.append(ahead)
        even.append(first * (1.0 / 65535.0))
        odd.append(second * (1.0 / 65535.0))
    out[0] = jnp.where(low, even[0], pltpu.roll(even[1], 4, 0))
    out[1] = jnp.where(low, odd[0], pltpu.roll(odd[1], 4, 0))
    out[2] = jnp.where(low, pltpu.roll(even[0], 4, 0), even[1])
    out[3] = 1.0 - jnp.where(low, passed[0], passed[1])


def local(bricks, levels, counts, gains, ownership, tf_slope):
    depth_count = lax.axis_size("depth")
    tile_count = lax.axis_size("tile")
    y_count = min(8, tile_count)
    x_count = tile_count // y_count
    vmem = pl.BlockSpec(memory_space=pltpu.VMEM)
    anywhere = pl.BlockSpec(memory_space=pltpu.HBM)
    dma = pltpu.SemaphoreType.DMA
    composite, share = pl.pallas_call(
        functools.partial(kernel, depth_count, x_count, y_count),
        out_shape=(
            pltpu.VMEM((4, 8, 128), F32),
            pltpu.VMEM((1, 1), F32),
        ),
        in_specs=[anywhere] * 6,
        out_specs=(vmem, vmem),
        scratch_shapes=[
            pltpu.SMEM((1, 16), I32),
            pltpu.SMEM((1, 16), F32),
            pltpu.SMEM((3,), F32),
            pltpu.VMEM((16, tile_count), I32),
            pltpu.VMEM((16, 32, 1024), BF16),
            pltpu.VMEM((8, 16, 128), I32),
            pltpu.VMEM((256, 768), BF16),
            pltpu.VMEM((768, 1024), BF16),
            pltpu.VMEM((512, 1024), BF16),
            pltpu.VMEM((2, 256, 256), BF16),
            pltpu.VMEM((2, 256, 1024), F32),
            pltpu.VMEM((2, 8, 8, 128), I32),
            pltpu.VMEM((2, 16, 8, 128), I32),
            pltpu.VMEM((8, 128), I32),
            pltpu.VMEM((8, 128), I32),
            pltpu.VMEM((x_count, 8, 128), I32),
            pltpu.VMEM((y_count, 8, 128), I32),
            pltpu.VMEM((2, 16, 8, 128), I32),
            dma((4,)),
            dma((4,)),
            dma((8,)),
            dma((2,)),
            dma((2,)),
            dma((2,)),
            dma((2,)),
            pltpu.SemaphoreType.REGULAR,
            pltpu.SemaphoreType.REGULAR,
            pltpu.SemaphoreType.REGULAR,
        ],
        compiler_params=pltpu.CompilerParams(
            collective_id=0, has_side_effects=True, vmem_limit_bytes=56000 * 1024
        ),
        name="render",
    )(bricks, levels, counts, gains, jnp.swapaxes(ownership, 1, 2), tf_slope)
    return composite.reshape(4, 1, 1024), share


def solution(mesh):
    placed = (
        P("depth", "tile", None, None),
        P("depth", "tile"),
        P("depth", "tile", None),
        P("depth", "tile"),
        P("depth", None, None),
        P(),
    )
    return jax.shard_map(
        local,
        mesh=mesh,
        in_specs=placed,
        out_specs=(P(None, "depth", "tile"), P("depth", "tile")),
        check_vma=False,
    )
```

```python
import functools

import jax
import jax.numpy as jnp
from jax import lax
from jax.experimental import pallas as pl
from jax.experimental.pallas import tpu as pltpu
from jax.sharding import PartitionSpec as P

F32 = jnp.float32
BF16 = jnp.bfloat16
I32 = jnp.int32
MESH = pl.DeviceIdType.MESH
CODE_FLOOR = -20.75
LOG2_E = 1.4426950408889634
LN_2 = 0.6931471805599453
CODE_SCALE = 65535.0 / 23.75


def tent(at, cell):
    return jnp.maximum(0.0, 1.0 - jnp.abs(at - cell))


def coarse_at(fine, side):
    return jnp.clip((fine + 0.5) * (side / 32.0) - 0.5, 0.0, side - 1.0)


def fill_plane_maps(maps):
    lane = lax.broadcasted_iota(I32, (8, 1024), 1)
    y_of = (lane // 32).astype(F32)
    x_of = lax.broadcasted_iota(I32, (32, 128), 1) % 32
    e_of = lax.broadcasted_iota(I32, (32, 128), 0).astype(F32)
    for first, side in ((0, 8), (256, 16)):
        along_x = tent(coarse_at(x_of.astype(F32), side), e_of)
        along_x = jnp.concatenate([along_x] * 8, axis=1)
        y_at = coarse_at(y_of, side)

        def one(c, carry, first=first, along_x=along_x, y_at=y_at):
            along_y = tent(y_at, c.astype(F32))
            both = along_x * jnp.concatenate([along_y] * 4, axis=0)
            maps[pl.ds(pl.multiple_of(first + c * 32, 32), 32), :] = both.astype(BF16)
            return carry

        lax.fori_loop(0, side, one, 0)


def brick_of(slot):
    half, place = slot // 8, slot % 8
    return 8 * half + 2 * (place % 4) + place // 4


def depth_map(levels, half):
    lane = lax.broadcasted_iota(I32, (1, 256), 1)
    slot = lane // 32
    grade = jnp.zeros((1, 256), I32)
    for s in range(8):
        grade = jnp.where(slot == s, levels[0, brick_of(8 * half + s)], grade)
    side = jnp.where(grade == 2, 32.0, jnp.where(grade == 1, 16.0, 8.0))
    cell = lane % 32
    cell = jnp.where(grade == 2, cell, cell % 16).astype(F32)
    row = lax.broadcasted_iota(I32, (256, 256), 0)
    z_of = (row // 8).astype(F32)
    at = jnp.minimum(jnp.maximum((z_of + 0.5) * (side / 32.0) - 0.5, 0.0), side - 1.0)
    same = (row % 8) == (lax.broadcasted_iota(I32, (256, 256), 1) // 32)
    return jnp.where(same, tent(at, cell), 0.0).astype(BF16)


def encode(tau, solid, sums):
    scale = 32767.5 / jnp.maximum(solid, 1e-12)
    codes = [
        jnp.clip(sums[k] * scale + 32768.0, 0.0, 65535.0).astype(I32) for k in range(3)
    ]
    depth = jnp.log2(jnp.maximum(tau * -LN_2, 1e-12))
    codes.append(jnp.clip((depth - CODE_FLOOR) * CODE_SCALE + 0.5, 0.0, 65535.0).astype(I32))
    return codes[0] | (codes[1] << 16), codes[2] | (codes[3] << 16)


def swapped(place):
    return place + 1 - 2 * (place % 2)


def wait_for(semaphore, count):
    @pl.when(count > 0)
    def _():
        pl.semaphore_wait(semaphore, count)


def y_order(y, count):
    back = count - y
    return jnp.where(y <= back, jnp.maximum(2 * y - 1, 0), 2 * back)


def y_at(order, count):
    return jnp.where(order % 2 == 1, (order + 1) // 2, (count - order // 2) % count)


def kernel(
    depth_count, x_count, y_count,
    bricks, levels_in, counts, gains_in, owners_in, slope_in,
    out, share,
    levels, gains, slope, owners,
    raw, lives, masked, maps, cells, zmaps, dens, shaded, sends,
    row_send, block_send, x_rows, y_rows, boxes,
    small_sem, brick_sem, live_sem, send_sem, box_sem,
    row_sem, row_box, depth_ready, x_ready, y_ready,
):
    me = lax.axis_index("depth")
    tile = lax.axis_index("tile")
    tile_count = x_count * y_count
    my_x, my_y = tile // y_count, tile % y_count

    fetch_small = [
        pltpu.make_async_copy(there, here, small_sem.at[i])
        for i, (there, here) in enumerate(
            ((levels_in, levels), (gains_in, gains), (slope_in, slope), (owners_in.at[0], owners))
        )
    ]
    fetch_bricks = [
        pltpu.make_async_copy(bricks.at[0, pl.ds(i * 4, 4)], raw.at[pl.ds(i * 4, 4)], brick_sem.at[i])
        for i in range(4)
    ]
    fetch_lives = [
        pltpu.make_async_copy(counts.at[0, :, pl.ds(j * 128, 128)], lives.at[j], live_sem.at[j])
        for j in range(8)
    ]
    for copy in fetch_bricks + fetch_small + fetch_lives:
        copy.start()

    barrier = pltpu.get_barrier_semaphore()
    order = swapped(me)

    def greet(peer, carry):
        pl.semaphore_signal(barrier, inc=1, device_id={"depth": swapped(peer)}, device_id_type=MESH)
        return carry

    lax.fori_loop(order + 1, depth_count, greet, 0)
    my_order = y_order(my_y, y_count)

    def at_x(x):
        return {"tile": x * y_count + my_y}

    def at_y(place):
        return {"tile": my_x * y_count + y_at(place, y_count)}

    def signal(semaphore, device):
        def one(peer, carry):
            pl.semaphore_signal(semaphore, inc=1, device_id=device(peer), device_id_type=MESH)
            return carry

        return one

    lax.fori_loop(my_x + 1, x_count, signal(barrier, at_x), 0)
    lax.fori_loop(my_order + 1, y_count, signal(barrier, at_y), 0)

    fill_plane_maps(maps)
    for copy in fetch_small:
        copy.wait()
    for half in range(2):
        zmaps[half] = depth_map(levels, half)

    for copy in fetch_bricks:
        copy.wait()
    for slot in range(16):
        b = brick_of(slot)
        grade = levels[0, b]
        rows = pl.ds(slot * 16, 16)
        for first, width, wanted in ((0, 256, 0), (256, 512, 1)):
            keep = jnp.full((16, width), jnp.where(grade == wanted, 1.0, 0.0), F32).astype(BF16)
            masked[rows, first : first + width] = raw[b, 0:16, 0:width] * keep

    for n in range(4):
        lanes = pl.ds(n * 256, 256)
        plane = jnp.dot(masked[...], maps[:, lanes], preferred_element_type=F32)
        high = plane.astype(BF16)
        low = (plane - high.astype(F32)).astype(BF16)
        for slot in range(16):
            b = brick_of(slot)
            keep = jnp.full((16, 256), jnp.where(levels[0, b] == 2, 1.0, 0.0), F32).astype(BF16)
            here = slice(slot * 16, slot * 16 + 16)
            cells[pl.ds(slot * 32, 16), lanes] = raw[b, 0:16, lanes] * keep + high[here]
            cells[pl.ds(slot * 32 + 16, 16), lanes] = raw[b, 16:32, lanes] * keep + low[here]

    for half in range(2):
        for n in range(4):
            lanes = pl.ds(n * 256, 256)
            dens[half, :, lanes] = jnp.dot(
                zmaps[half], cells[pl.ds(half * 256, 256), lanes], preferred_element_type=F32
            )

    sub = lax.broadcasted_iota(I32, (8, 128), 0)
    lane = lax.broadcasted_iota(I32, (8, 128), 1)
    for copy in fetch_lives:
        copy.wait()
    slopes = [slope[k] * 0.5 for k in range(3)]

    def pixels(half, to):
        return pltpu.make_async_remote_copy(
            src_ref=sends.at[half, to], dst_ref=boxes.at[half, me],
            send_sem=send_sem.at[half], recv_sem=box_sem.at[half],
            device_id={"depth": to}, device_id_type=MESH,
        )

    def send(half, peer, carry):
        pixels(half, swapped(peer)).start()
        return carry

    def along_x(x):
        return pltpu.make_async_remote_copy(
            src_ref=row_send, dst_ref=x_rows.at[my_x], send_sem=row_sem.at[0], recv_sem=row_box.at[0],
            device_id=at_x(x), device_id_type=MESH,
        )

    def along_y(place):
        return pltpu.make_async_remote_copy(
            src_ref=block_send, dst_ref=y_rows.at[my_y], send_sem=row_sem.at[1], recv_sem=row_box.at[1],
            device_id=at_y(place), device_id_type=MESH,
        )

    def start(copy):
        def one(peer, carry):
            copy(peer).start()
            return carry

        return one

    def take(buffer, count, semaphore):
        if count:
            some = buffer.at[pl.ds(0, count)]
            pltpu.make_async_copy(some, some, semaphore).wait()

    packed = jnp.zeros((8, 128), I32)
    for s in range(8):
        packed = jnp.where(sub == s, levels[0, s] + 256 * levels[0, s + 8], packed)
    row_send[...] = packed
    x_rows[my_x] = packed

    source = (lane % 8) * 16 + (lane // 8 % 8) * 2 + lane // 64

    for half in range(2):
        gain = jnp.zeros((8, 128), F32)
        for s in range(8):
            gain = jnp.where(sub == s, -gains[0, brick_of(8 * half + s)], gain)

        gain = jnp.concatenate([gain, gain], axis=1)

        def shade(n, carry, half=half, gain=gain):
            lanes = pl.ds(pl.multiple_of(n * 256, 256), 256)
            live = jnp.concatenate(
                [
                    jnp.concatenate(
                        [lives[2 * n + j, pl.ds(8 * half + odd, 4, stride=2), :] for odd in range(2)], axis=0
                    )
                    for j in range(2)
                ],
                axis=1,
            )
            tau = jnp.zeros((8, 256), F32)
            through = jnp.ones((8, 256), F32)
            sums = [jnp.zeros((8, 256), F32)] * 3
            for z in range(32):
                x = dens[half, z * 8 : z * 8 + 8, lanes]
                soft = jnp.log2(1.0 + jnp.exp2(x * LOG2_E))
                tau = tau + jnp.where(live > z, soft * gain, 0.0)
                after = jnp.exp2(tau)
                glow = through - after
                through = after
                for k in range(3):
                    sums[k] = sums[k] + glow * jnp.tanh(x * slopes[k])
            for k, words in enumerate(encode(tau, 1.0 - through, sums)):
                for j in range(2):
                    shaded[k, 2 * n + j] = words[:, 128 * j : 128 * j + 128]
            return carry

        lax.fori_loop(0, 4, shade, 0)

        kinds = []
        for kind in range(2):
            parts = []
            for j in range(8):
                first, second = shaded[0, j], shaded[1, j]
                if kind == 0:
                    words = jnp.where(sub < 4, first, pltpu.roll(second, 4, 0))
                else:
                    words = jnp.where(sub < 4, pltpu.roll(first, 4, 0), second)
                parts.append(jnp.take_along_axis(words, source, axis=1, mode="promise_in_bounds"))
            for bit in range(3):
                step = 1 << bit
                upper = (lane // (8 * step)) % 2 == 1
                for j in range(8):
                    if j & step:
                        continue
                    a, b = parts[j], parts[j + step]
                    parts[j] = jnp.where(upper, pltpu.roll(b, 8 * step, 1), a)
                    parts[j + step] = jnp.where(upper, b, pltpu.roll(a, 128 - 8 * step, 1))
            kinds.append(parts)
        for g in range(8):
            even, odd = kinds[0][g], kinds[1][g]
            sends[half, 2 * g] = jnp.where(lane < 64, even, pltpu.roll(odd, 64, 1))
            sends[half, 2 * g + 1] = jnp.where(lane < 64, pltpu.roll(even, 64, 1), odd)

        if half == 0:
            wait_for(barrier, order + my_x + my_order)
            lax.fori_loop(0, my_x, signal(x_ready, at_x), 0)
            lax.fori_loop(0, my_x, start(along_x), 0)
            lax.fori_loop(0, my_order, signal(y_ready, at_y), 0)
        lax.fori_loop(0, order, functools.partial(send, half), 0)
        boxes[half, me] = sends[half, me]
        if half == 0:
            lax.fori_loop(0, order, signal(depth_ready, lambda peer: {"depth": swapped(peer)}), 0)

    def serve_later():
        wait_for(depth_ready, depth_count - 1 - order)
        for half in range(2):
            lax.fori_loop(order + 1, depth_count, functools.partial(send, half), 0)

    wait_for(x_ready, x_count - 1 - my_x)
    lax.fori_loop(my_x + 1, x_count, start(along_x), 0)
    pl.when(me >= depth_count // 2)(serve_later)
    take(x_rows, x_count - 1, row_box.at[0])
    table = jnp.zeros((8, 128), I32)
    for x in range(x_count):
        table = jnp.where(lane // y_count == x, x_rows[x], table)
    block_send[...] = table
    y_rows[my_y] = table
    wait_for(y_ready, y_count - 1 - my_order)
    lax.fori_loop(0, my_order, start(along_y), 0)
    lax.fori_loop(my_order + 1, y_count, start(along_y), 0)
    pl.when(me < depth_count // 2)(serve_later)
    take(y_rows, y_count - 1, row_box.at[1])
    for y in range(y_count):
        table = jnp.where(lane % y_count == y, y_rows[y], table)
    table = table[:, 0:tile_count]
    total = jnp.zeros((8, tile_count), F32)
    for part, grade in enumerate((table & 255, table >> 8)):
        worth = jnp.where(grade == 2, 1.0, jnp.where(grade == 1, 0.25, 0.0625))
        total = total + jnp.where(owners[8 * part : 8 * part + 8] == tile, worth, 0.0)
    share[...] = jnp.sum(total, keepdims=True) * (1.0 / 16.0)

    take(x_rows, x_count - 1, row_sem.at[0])
    take(y_rows, y_count - 1, row_sem.at[1])
    for half in range(2):
        take(sends.at[half], depth_count - 1, send_sem.at[half])
    low = lax.broadcasted_iota(I32, (8, 128), 0) < 4
    passed, even, odd = [], [], []
    for half in range(2):
        take(boxes.at[half], depth_count - 1, box_sem.at[half])
        ahead = jnp.ones((8, 128), F32)
        first = jnp.zeros((8, 128), F32)
        second = jnp.zeros((8, 128), F32)
        for d in range(depth_count):
            word = boxes[half, d]
            bottom = (word & 65535).astype(F32)
            top = lax.shift_right_logical(word, 16).astype(F32)
            code = jnp.where(low, pltpu.roll(top, 4, 0), top)
            through = jnp.exp(-jnp.exp2(code * (1.0 / CODE_SCALE) + CODE_FLOOR))
            weight = ahead * (1.0 - through)
            first = first + weight * bottom
            second = second + weight * top
            ahead = ahead * through
        passed.append(ahead)
        even.append(first * (1.0 / 65535.0))
        odd.append(second * (1.0 / 65535.0))
    out[0] = jnp.where(low, even[0], pltpu.roll(even[1], 4, 0))
    out[1] = jnp.where(low, odd[0], pltpu.roll(odd[1], 4, 0))
    out[2] = jnp.where(low, pltpu.roll(even[0], 4, 0), even[1])
    out[3] = 1.0 - jnp.where(low, passed[0], passed[1])


def local(bricks, levels, counts, gains, ownership, tf_slope):
    depth_count = lax.axis_size("depth")
    tile_count = lax.axis_size("tile")
    y_count = min(8, tile_count)
    x_count = tile_count // y_count
    vmem = pl.BlockSpec(memory_space=pltpu.VMEM)
    anywhere = pl.BlockSpec(memory_space=pltpu.HBM)
    dma = pltpu.SemaphoreType.DMA
    composite, share = pl.pallas_call(
        functools.partial(kernel, depth_count, x_count, y_count),
        out_shape=(
            pltpu.VMEM((4, 8, 128), F32),
            pltpu.VMEM((1, 1), F32),
        ),
        in_specs=[anywhere] * 6,
        out_specs=(vmem, vmem),
        scratch_shapes=[
            pltpu.SMEM((1, 16), I32),
            pltpu.SMEM((1, 16), F32),
            pltpu.SMEM((3,), F32),
            pltpu.VMEM((16, tile_count), I32),
            pltpu.VMEM((16, 32, 1024), BF16),
            pltpu.VMEM((8, 16, 128), I32),
            pltpu.VMEM((256, 768), BF16),
            pltpu.VMEM((768, 1024), BF16),
            pltpu.VMEM((512, 1024), BF16),
            pltpu.VMEM((2, 256, 256), BF16),
            pltpu.VMEM((2, 256, 1024), F32),
            pltpu.VMEM((2, 8, 8, 128), I32),
            pltpu.VMEM((2, 16, 8, 128), I32),
            pltpu.VMEM((8, 128), I32),
            pltpu.VMEM((8, 128), I32),
            pltpu.VMEM((x_count, 8, 128), I32),
            pltpu.VMEM((y_count, 8, 128), I32),
            pltpu.VMEM((2, 16, 8, 128), I32),
            dma((4,)),
            dma((4,)),
            dma((8,)),
            dma((2,)),
            dma((2,)),
            dma((2,)),
            dma((2,)),
            pltpu.SemaphoreType.REGULAR,
            pltpu.SemaphoreType.REGULAR,
            pltpu.SemaphoreType.REGULAR,
        ],
        compiler_params=pltpu.CompilerParams(
            collective_id=0, has_side_effects=True, vmem_limit_bytes=56000 * 1024
        ),
        name="render",
    )(bricks, levels, counts, gains, jnp.swapaxes(ownership, 1, 2), tf_slope)
    return composite.reshape(4, 1, 1024), share


def solution(mesh):
    placed = (
        P("depth", "tile", None, None),
        P("depth", "tile"),
        P("depth", "tile", None),
        P("depth", "tile"),
        P("depth", None, None),
        P(),
    )
    return jax.shard_map(
        local,
        mesh=mesh,
        in_specs=placed,
        out_specs=(P(None, "depth", "tile"), P("depth", "tile")),
        check_vma=False,
    )
```

```python
import functools

import jax
import jax.numpy as jnp
from jax import lax
from jax.experimental import pallas as pl
from jax.experimental.pallas import tpu as pltpu
from jax.sharding import PartitionSpec as P

F32 = jnp.float32
BF16 = jnp.bfloat16
I32 = jnp.int32
MESH = pl.DeviceIdType.MESH
CODE_FLOOR = -20.75
LOG2_E = 1.4426950408889634
LN_2 = 0.6931471805599453
CODE_SCALE = 65535.0 / 23.75


def tent(at, cell):
    return jnp.maximum(0.0, 1.0 - jnp.abs(at - cell))


def coarse_at(fine, side):
    return jnp.clip((fine + 0.5) * (side / 32.0) - 0.5, 0.0, side - 1.0)


def fill_plane_maps(maps):
    lane = lax.broadcasted_iota(I32, (8, 1024), 1)
    y_of = (lane // 32).astype(F32)
    x_of = lax.broadcasted_iota(I32, (32, 128), 1) % 32
    e_of = lax.broadcasted_iota(I32, (32, 128), 0).astype(F32)
    for first, side in ((0, 8), (256, 16)):
        along_x = tent(coarse_at(x_of.astype(F32), side), e_of)
        along_x = jnp.concatenate([along_x] * 8, axis=1)
        y_at = coarse_at(y_of, side)

        def one(c, carry, first=first, along_x=along_x, y_at=y_at):
            along_y = tent(y_at, c.astype(F32))
            both = along_x * jnp.concatenate([along_y] * 4, axis=0)
            maps[pl.ds(pl.multiple_of(first + c * 32, 32), 32), :] = both.astype(BF16)
            return carry

        lax.fori_loop(0, side, one, 0)


def brick_of(slot):
    half, place = slot // 8, slot % 8
    return 8 * half + 2 * (place % 4) + place // 4


def depth_map(levels, half):
    lane = lax.broadcasted_iota(I32, (1, 256), 1)
    slot = lane // 32
    grade = jnp.zeros((1, 256), I32)
    for s in range(8):
        grade = jnp.where(slot == s, levels[0, brick_of(8 * half + s)], grade)
    side = jnp.where(grade == 2, 32.0, jnp.where(grade == 1, 16.0, 8.0))
    cell = lane % 32
    cell = jnp.where(grade == 2, cell, cell % 16).astype(F32)
    row = lax.broadcasted_iota(I32, (256, 256), 0)
    z_of = (row // 8).astype(F32)
    at = jnp.minimum(jnp.maximum((z_of + 0.5) * (side / 32.0) - 0.5, 0.0), side - 1.0)
    same = (row % 8) == (lax.broadcasted_iota(I32, (256, 256), 1) // 32)
    return jnp.where(same, tent(at, cell), 0.0).astype(BF16)


def encode(tau, solid, sums):
    scale = 32767.5 / jnp.maximum(solid, 1e-12)
    codes = [
        jnp.clip(sums[k] * scale + 32768.0, 0.0, 65535.0).astype(I32) for k in range(3)
    ]
    depth = jnp.log2(jnp.maximum(tau * -LN_2, 1e-12))
    codes.append(jnp.clip((depth - CODE_FLOOR) * CODE_SCALE + 0.5, 0.0, 65535.0).astype(I32))
    return codes[0] | (codes[1] << 16), codes[2] | (codes[3] << 16)


def swapped(place):
    return place + 1 - 2 * (place % 2)


def wait_for(semaphore, count):
    @pl.when(count > 0)
    def _():
        pl.semaphore_wait(semaphore, count)


def y_order(y, count):
    back = count - y
    return jnp.where(y <= back, jnp.maximum(2 * y - 1, 0), 2 * back)


def y_at(order, count):
    return jnp.where(order % 2 == 1, (order + 1) // 2, (count - order // 2) % count)


def kernel(
    depth_count, x_count, y_count,
    bricks, levels_in, counts, gains_in, owners_in, slope_in,
    out, share,
    levels, gains, slope, owners,
    raw, lives, masked, maps, cells, zmaps, dens, shaded, sends,
    row_send, block_send, x_rows, y_rows, boxes,
    small_sem, brick_sem, live_sem, send_sem, box_sem,
    row_sem, row_box, depth_ready, x_ready, y_ready,
):
    me = lax.axis_index("depth")
    tile = lax.axis_index("tile")
    tile_count = x_count * y_count
    my_x, my_y = tile // y_count, tile % y_count

    fetch_small = [
        pltpu.make_async_copy(there, here, small_sem.at[i])
        for i, (there, here) in enumerate(
            ((levels_in, levels), (gains_in, gains), (slope_in, slope), (owners_in.at[0], owners))
        )
    ]
    fetch_bricks = [
        pltpu.make_async_copy(bricks.at[0, pl.ds(i * 4, 4)], raw.at[pl.ds(i * 4, 4)], brick_sem.at[i])
        for i in range(4)
    ]
    fetch_lives = [
        pltpu.make_async_copy(counts.at[0, :, pl.ds(j * 128, 128)], lives.at[j, pl.ds(0, 16)], live_sem.at[j])
        for j in range(8)
    ]
    for copy in fetch_bricks + fetch_small + fetch_lives:
        copy.start()

    barrier = pltpu.get_barrier_semaphore()
    order = swapped(me)

    def greet(peer, carry):
        pl.semaphore_signal(barrier, inc=1, device_id={"depth": swapped(peer)}, device_id_type=MESH)
        return carry

    lax.fori_loop(order + 1, depth_count, greet, 0)
    my_order = y_order(my_y, y_count)

    def at_x(x):
        return {"tile": x * y_count + my_y}

    def at_y(place):
        return {"tile": my_x * y_count + y_at(place, y_count)}

    def signal(semaphore, device):
        def one(peer, carry):
            pl.semaphore_signal(semaphore, inc=1, device_id=device(peer), device_id_type=MESH)
            return carry

        return one

    lax.fori_loop(my_x + 1, x_count, signal(barrier, at_x), 0)
    lax.fori_loop(my_order + 1, y_count, signal(barrier, at_y), 0)

    fill_plane_maps(maps)
    for copy in fetch_small:
        copy.wait()
    for half in range(2):
        zmaps[half] = depth_map(levels, half)

    for copy in fetch_bricks:
        copy.wait()
    for slot in range(16):
        b = brick_of(slot)
        grade = levels[0, b]
        rows = pl.ds(slot * 16, 16)
        for first, width, wanted in ((0, 256, 0), (256, 512, 1)):
            keep = jnp.full((16, width), jnp.where(grade == wanted, 1.0, 0.0), F32).astype(BF16)
            masked[rows, first : first + width] = raw[b, 0:16, 0:width] * keep

    for n in range(4):
        lanes = pl.ds(n * 256, 256)
        plane = jnp.dot(masked[...], maps[:, lanes], preferred_element_type=F32)
        high = plane.astype(BF16)
        low = (plane - high.astype(F32)).astype(BF16)
        for slot in range(16):
            b = brick_of(slot)
            keep = jnp.full((16, 256), jnp.where(levels[0, b] == 2, 1.0, 0.0), F32).astype(BF16)
            here = slice(slot * 16, slot * 16 + 16)
            cells[pl.ds(slot * 32, 16), lanes] = raw[b, 0:16, lanes] * keep + high[here]
            cells[pl.ds(slot * 32 + 16, 16), lanes] = raw[b, 16:32, lanes] * keep + low[here]

    for half in range(2):
        for n in range(4):
            lanes = pl.ds(n * 256, 256)
            dens[half, :, lanes] = jnp.dot(
                zmaps[half], cells[pl.ds(half * 256, 256), lanes], preferred_element_type=F32
            )

    sub = lax.broadcasted_iota(I32, (8, 128), 0)
    lane = lax.broadcasted_iota(I32, (8, 128), 1)
    for copy in fetch_lives:
        copy.wait()
    slopes = [slope[k] * 0.5 for k in range(3)]

    def pixels(half, to):
        return pltpu.make_async_remote_copy(
            src_ref=sends.at[half, to], dst_ref=boxes.at[half, me],
            send_sem=send_sem.at[half], recv_sem=box_sem.at[half],
            device_id={"depth": to}, device_id_type=MESH,
        )

    def send(half, peer, carry):
        pixels(half, swapped(peer)).start()
        return carry

    def along_x(x):
        return pltpu.make_async_remote_copy(
            src_ref=row_send, dst_ref=x_rows.at[my_x], send_sem=row_sem.at[0], recv_sem=row_box.at[0],
            device_id=at_x(x), device_id_type=MESH,
        )

    def along_y(place):
        return pltpu.make_async_remote_copy(
            src_ref=block_send, dst_ref=y_rows.at[my_y], send_sem=row_sem.at[1], recv_sem=row_box.at[1],
            device_id=at_y(place), device_id_type=MESH,
        )

    def start(copy):
        def one(peer, carry):
            copy(peer).start()
            return carry

        return one

    def take(buffer, count, semaphore):
        if count:
            some = buffer.at[pl.ds(0, count)]
            pltpu.make_async_copy(some, some, semaphore).wait()

    packed = jnp.zeros((8, 128), I32)
    for s in range(8):
        packed = jnp.where(sub == s, levels[0, s] + 256 * levels[0, s + 8], packed)
    row_send[...] = packed
    x_rows[my_x] = packed

    source = (lane % 8) * 16 + (lane // 8 % 8) * 2 + lane // 64

    for half in range(2):
        gain = jnp.zeros((8, 128), F32)
        for s in range(8):
            gain = jnp.where(sub == s, -gains[0, brick_of(8 * half + s)], gain)

        gain = jnp.concatenate([gain, gain], axis=1)

        def shade(n, carry, half=half, gain=gain):
            lanes = pl.ds(pl.multiple_of(n * 256, 256), 256)
            live = jnp.concatenate(
                [
                    jnp.concatenate(
                        [lives[2 * n + j, pl.ds(8 * half + odd, 4, stride=2), :] for odd in range(2)], axis=0
                    )
                    for j in range(2)
                ],
                axis=1,
            )
            tau = jnp.zeros((8, 256), F32)
            through = jnp.ones((8, 256), F32)
            sums = [jnp.zeros((8, 256), F32)] * 3
            for z in range(32):
                x = dens[half, z * 8 : z * 8 + 8, lanes]
                soft = jnp.log2(1.0 + jnp.exp2(x * LOG2_E))
                tau = tau + jnp.where(live > z, soft * gain, 0.0)
                after = jnp.exp2(tau)
                glow = through - after
                through = after
                for k in range(3):
                    sums[k] = sums[k] + glow * jnp.tanh(x * slopes[k])
            for k, words in enumerate(encode(tau, 1.0 - through, sums)):
                for j in range(2):
                    shaded[k, 2 * n + j] = words[:, 128 * j : 128 * j + 128]
            return carry

        lax.fori_loop(0, 4, shade, 0)

        kinds = []
        for kind in range(2):
            parts = []
            for j in range(8):
                first, second = shaded[0, j], shaded[1, j]
                if kind == 0:
                    words = jnp.where(sub < 4, first, pltpu.roll(second, 4, 0))
                else:
                    words = jnp.where(sub < 4, pltpu.roll(first, 4, 0), second)
                parts.append(jnp.take_along_axis(words, source, axis=1, mode="promise_in_bounds"))
            for bit in range(3):
                step = 1 << bit
                upper = (lane // (8 * step)) % 2 == 1
                for j in range(8):
                    if j & step:
                        continue
                    a, b = parts[j], parts[j + step]
                    parts[j] = jnp.where(upper, pltpu.roll(b, 8 * step, 1), a)
                    parts[j + step] = jnp.where(upper, b, pltpu.roll(a, 128 - 8 * step, 1))
            kinds.append(parts)
        for g in range(8):
            even, odd = kinds[0][g], kinds[1][g]
            sends[half, 2 * g] = jnp.where(lane < 64, even, pltpu.roll(odd, 64, 1))
            sends[half, 2 * g + 1] = jnp.where(lane < 64, pltpu.roll(even, 64, 1), odd)

        if half == 0:
            wait_for(barrier, order + my_x + my_order)
            lax.fori_loop(0, my_x, signal(x_ready, at_x), 0)
            lax.fori_loop(0, my_x, start(along_x), 0)
            lax.fori_loop(0, my_order, signal(y_ready, at_y), 0)
        lax.fori_loop(0, order, functools.partial(send, half), 0)
        boxes[half, me] = sends[half, me]
        if half == 0:
            lax.fori_loop(0, order, signal(depth_ready, lambda peer: {"depth": swapped(peer)}), 0)

    def serve_later():
        wait_for(depth_ready, depth_count - 1 - order)
        for half in range(2):
            lax.fori_loop(order + 1, depth_count, functools.partial(send, half), 0)

    wait_for(x_ready, x_count - 1 - my_x)
    lax.fori_loop(my_x + 1, x_count, start(along_x), 0)
    pl.when(me >= depth_count // 2)(serve_later)
    take(x_rows, x_count - 1, row_box.at[0])
    table = jnp.zeros((8, 128), I32)
    for x in range(x_count):
        table = jnp.where(lane // y_count == x, x_rows[x], table)
    block_send[...] = table
    y_rows[my_y] = table
    wait_for(y_ready, y_count - 1 - my_order)
    lax.fori_loop(0, my_order, start(along_y), 0)
    lax.fori_loop(my_order + 1, y_count, start(along_y), 0)
    pl.when(me < depth_count // 2)(serve_later)
    take(y_rows, y_count - 1, row_box.at[1])
    for y in range(y_count):
        table = jnp.where(lane % y_count == y, y_rows[y], table)
    table = table[:, 0:tile_count]
    total = jnp.zeros((8, tile_count), F32)
    for part, grade in enumerate((table & 255, table >> 8)):
        worth = jnp.where(grade == 2, 1.0, jnp.where(grade == 1, 0.25, 0.0625))
        total = total + jnp.where(owners[8 * part : 8 * part + 8] == tile, worth, 0.0)
    share[...] = jnp.sum(total, keepdims=True) * (1.0 / 16.0)

    take(x_rows, x_count - 1, row_sem.at[0])
    take(y_rows, y_count - 1, row_sem.at[1])
    for half in range(2):
        take(sends.at[half], depth_count - 1, send_sem.at[half])
    low = lax.broadcasted_iota(I32, (8, 128), 0) < 4
    passed, even, odd = [], [], []
    for half in range(2):
        take(boxes.at[half], depth_count - 1, box_sem.at[half])
        ahead = jnp.ones((8, 128), F32)
        first = jnp.zeros((8, 128), F32)
        second = jnp.zeros((8, 128), F32)
        for d in range(depth_count):
            word = boxes[half, d]
            bottom = (word & 65535).astype(F32)
            top = lax.shift_right_logical(word, 16).astype(F32)
            code = jnp.where(low, pltpu.roll(top, 4, 0), top)
            through = jnp.exp(-jnp.exp2(code * (1.0 / CODE_SCALE) + CODE_FLOOR))
            weight = ahead * (1.0 - through)
            first = first + weight * bottom
            second = second + weight * top
            ahead = ahead * through
        passed.append(ahead)
        even.append(first * (1.0 / 65535.0))
        odd.append(second * (1.0 / 65535.0))
    out[0] = jnp.where(low, even[0], pltpu.roll(even[1], 4, 0))
    out[1] = jnp.where(low, odd[0], pltpu.roll(odd[1], 4, 0))
    out[2] = jnp.where(low, pltpu.roll(even[0], 4, 0), even[1])
    out[3] = 1.0 - jnp.where(low, passed[0], passed[1])


def local(bricks, levels, counts, gains, ownership, tf_slope):
    depth_count = lax.axis_size("depth")
    tile_count = lax.axis_size("tile")
    y_count = min(8, tile_count)
    x_count = tile_count // y_count
    vmem = pl.BlockSpec(memory_space=pltpu.VMEM)
    anywhere = pl.BlockSpec(memory_space=pltpu.HBM)
    dma = pltpu.SemaphoreType.DMA
    composite, share = pl.pallas_call(
        functools.partial(kernel, depth_count, x_count, y_count),
        out_shape=(
            pltpu.VMEM((4, 8, 128), F32),
            pltpu.VMEM((1, 1), F32),
        ),
        in_specs=[anywhere] * 6,
        out_specs=(vmem, vmem),
        scratch_shapes=[
            pltpu.SMEM((1, 16), I32),
            pltpu.SMEM((1, 16), F32),
            pltpu.SMEM((3,), F32),
            pltpu.VMEM((16, tile_count), I32),
            pltpu.VMEM((16, 32, 1024), BF16),
            pltpu.VMEM((8, 24, 128), I32),
            pltpu.VMEM((256, 768), BF16),
            pltpu.VMEM((768, 1024), BF16),
            pltpu.VMEM((512, 1024), BF16),
            pltpu.VMEM((2, 256, 256), BF16),
            pltpu.VMEM((2, 256, 1024), F32),
            pltpu.VMEM((2, 8, 8, 128), I32),
            pltpu.VMEM((2, 16, 8, 128), I32),
            pltpu.VMEM((8, 128), I32),
            pltpu.VMEM((8, 128), I32),
            pltpu.VMEM((x_count, 8, 128), I32),
            pltpu.VMEM((y_count, 8, 128), I32),
            pltpu.VMEM((2, 16, 8, 128), I32),
            dma((4,)),
            dma((4,)),
            dma((8,)),
            dma((2,)),
            dma((2,)),
            dma((2,)),
            dma((2,)),
            pltpu.SemaphoreType.REGULAR,
            pltpu.SemaphoreType.REGULAR,
            pltpu.SemaphoreType.REGULAR,
        ],
        compiler_params=pltpu.CompilerParams(
            collective_id=0, has_side_effects=True, vmem_limit_bytes=56000 * 1024
        ),
        name="render",
    )(bricks, levels, counts, gains, jnp.swapaxes(ownership, 1, 2), tf_slope)
    return composite.reshape(4, 1, 1024), share


def solution(mesh):
    placed = (
        P("depth", "tile", None, None),
        P("depth", "tile"),
        P("depth", "tile", None),
        P("depth", "tile"),
        P("depth", None, None),
        P(),
    )
    return jax.shard_map(
        local,
        mesh=mesh,
        in_specs=placed,
        out_specs=(P(None, "depth", "tile"), P("depth", "tile")),
        check_vma=False,
    )
```
